768 devices in a mesh: dom: 12 (over z), inner: 64 (over x, y, core).
Axes of the slice: x: 4, y: 8, z: 12, core: 2. Of those that a mesh axis runs over, the one named last changes fastest.
Arguments:
- features: bfloat16 [786432, 256], P(('dom', 'inner')), may hold values from -6 to 6
- tiles: bfloat16 [6144, 8, 128, 128], P(('dom', 'inner')), may hold values from 0 to 1, as said below
- pair_source: int32 [6144, 8], P(('dom', 'inner')), may hold values from 0 to 21, as said below
- in_degree: int32 [786432], P(('dom', 'inner')), may hold values from 1 to 1056, as said below
- send_blocks: int32 [768, 12], P(('dom', 'inner')), may hold values from 0 to 7
- w_self: bfloat16 [256, 256], replicated, may hold values from -0.375 to 0.375
- w_neigh: bfloat16 [256, 256], replicated, may hold values from -3 to 3
- bias: float32 [256], replicated, may hold values from -3 to 3
- cotangent: bfloat16 [786432, 256], P(('dom', 'inner')), may hold values from -6 to 6
Outputs:
- layer_out: bfloat16 [786432, 256], P(('dom', 'inner'))
- grad_features: bfloat16 [786432, 256], P(('dom', 'inner'))
- grad_self: float32 [256, 256], replicated
- grad_neigh: float32 [256, 256], replicated
- grad_bias: float32 [256], replicated
The draws below stay inside these ranges and needn't reach their ends.
Inputs may be any that keep to these rules, and one draw needn't show every extreme that they name: `pair_source`: every device's 8 * 8 pairs name each of its 22 table entries at least once. `in_degree`: each node's in-degree is at least one more than the number of ones in its rows of its block's tiles. `tiles`: entries are 0 or 1.
All inputs are finite; a program needn't handle non-finite values.
Results may differ from the reference program's by a relative error of at most 0.0075.
Values may be sent and summed in bfloat16 or wider, within the bound.
No kernel may reach another device: no remote copies, remote signals or barrier semaphores. Data moves between devices by JAX's collectives and lax.ppermute only.
A program may use at most 64 MiB of HBM per device.

```python
import jax
import jax.numpy as jnp
from jax import lax

F = 256
H = 256
BLOCK = 128
P_SIZE = 8
B_DEV = 8
BLOCKS = 6144
NODES = 786432
TABLE = 22
N_DOM = 12
N_INNER = 64
DEVICES = 768


def tile_mask(key):
    return jax.random.randint(key, (BLOCKS, P_SIZE, BLOCK, BLOCK), 0, 8) == 0


def draw_tiles(key, part):
    marked = tile_mask(key)
    return marked.astype(jnp.float32).astype(jnp.bfloat16)


def draw_in_degree(key, part):
    counts = tile_mask(key).astype(jnp.int32).sum(axis=(1, 3)).reshape(NODES)
    key = jax.random.fold_in(key, 2)
    spare_key, pick_key = jax.random.split(key)
    spare = jax.random.randint(spare_key, (NODES,), 1, 33)
    degree = (counts + spare).astype(jnp.int32)
    picked = jax.random.randint(pick_key, (), 0, NODES)
    return degree.at[picked].set(P_SIZE * BLOCK + 32).astype(jnp.int32)


def draw_pair_source(key, part):
    key = jax.random.fold_in(key, 3)
    device_keys = jax.random.split(key, DEVICES)

    def one_device(device_key):
        key_order, key_fill, key_mix = jax.random.split(device_key, 3)
        ordered = jax.random.permutation(key_order, TABLE).astype(jnp.int32)
        filler = jax.random.randint(key_fill, (B_DEV * P_SIZE - TABLE,), 0, TABLE).astype(jnp.int32)
        return jax.random.permutation(key_mix, jnp.concatenate([ordered, filler]))
    listed = jax.vmap(one_device)(device_keys)
    return listed.reshape(BLOCKS, P_SIZE).astype(jnp.int32)


def place_ends(values, own_key, least, high):
    dims = values.shape
    place = [jax.random.randint(jax.random.fold_in(own_key, axis), (), 0, dims[axis]) for axis in range(len(dims))]
    values = values.at[tuple(place)].set(least)
    longest = dims.index(max(dims))
    place[longest] = (place[longest] + 1) % dims[longest]
    return values.at[tuple(place)].set(high)


def block_levels(rng, shape, shards, smallest, high):
    loudness = 1.0
    for dim, parts in shards:
        steps = jax.random.uniform(jax.random.fold_in(jax.random.fold_in(rng, 6), dim), (parts,), jnp.float32, smallest / len(shards), high / len(shards))
        loudness = loudness * jnp.repeat(jnp.exp(steps), shape[dim] // parts).reshape((-1,) + (1,) * (len(shape) - 1 - dim))
    return loudness


def centred(own_key, dims, scale, reach, cuts=(), kind=jnp.bfloat16):
    level = block_levels(own_key, dims, cuts, -0.22, 0.18) if cuts else 1.0
    drawn = jax.random.normal(own_key, dims, jnp.float32) * scale * level
    return jnp.minimum(jnp.maximum(drawn, -reach), reach).astype(kind)


def setup_inputs(seed: int = 0) -> dict:
    keys = jax.random.split(jax.random.key(seed), 10)
    return {
        "features": centred(keys[0], (NODES, F), 1.0, 6.0, ((0, 768),)),
        "tiles": draw_tiles(jax.random.fold_in(keys[9], 71), 0),
        "pair_source": draw_pair_source(jax.random.fold_in(keys[9], 71), 0),
        "in_degree": draw_in_degree(jax.random.fold_in(keys[9], 71), 0),
        "send_blocks": place_ends(jax.random.randint(keys[4], (DEVICES, N_DOM), 0, B_DEV), jax.random.fold_in(keys[4], 1), 0, B_DEV - 1).astype(jnp.int32),
        "w_self": centred(keys[5], (F, H), F ** -0.5, 0.375),
        "w_neigh": centred(keys[6], (F, H), (F // 64) ** -0.5, 3.0),
        "bias": centred(keys[7], (H,), 0.5, 3.0, (), jnp.float32),
        "cotangent": centred(keys[8], (NODES, H), 1.0, 6.0, ((0, 768),)),
    }


def reference(features, tiles, pair_source, in_degree, send_blocks, w_self, w_neigh, bias, cotangent):
    width = features.shape[1]
    hidden = w_self.shape[1]
    devices = N_DOM * N_INNER
    rows_dev = B_DEV * BLOCK
    zero_id = devices * B_DEV
    blocks = features.reshape(zero_id, BLOCK, width)
    padded = jnp.concatenate([blocks, jnp.zeros((1, BLOCK, width), features.dtype)], axis=0)
    degree = in_degree.astype(jnp.float32).reshape(devices, rows_dev)
    tile_dev = tiles.reshape(devices, B_DEV, P_SIZE, BLOCK, BLOCK)
    pairs_dev = pair_source.reshape(devices, B_DEV * P_SIZE).astype(jnp.int32)
    feat_dev = features.reshape(devices, rows_dev, width)
    cot_dev = cotangent.reshape(devices, rows_dev, hidden)
    block_range = jnp.arange(B_DEV, dtype=jnp.int32)
    peer_range = jnp.arange(N_DOM, dtype=jnp.int32)

    def step(carry, device):
        grad_sum, sum_self, sum_neigh, sum_bias = carry
        dom_idx = device // N_INNER
        inner_idx = device % N_INNER
        own_ids = (device * B_DEV + block_range).astype(jnp.int32)
        left_id = jnp.where(inner_idx > 0, device * B_DEV - 1, zero_id).astype(jnp.int32)
        right_id = jnp.where(inner_idx < N_INNER - 1, (device + 1) * B_DEV, zero_id).astype(jnp.int32)
        peers = peer_range * N_INNER + inner_idx
        slot_ids = (peers * B_DEV + send_blocks[peers, dom_idx]).astype(jnp.int32)
        entry_ids = jnp.concatenate([own_ids, left_id[None], right_id[None], slot_ids]).astype(jnp.int32)
        source_table = padded[entry_ids]
        pairs = pairs_dev[device]
        sources = source_table[pairs].reshape(B_DEV, P_SIZE, BLOCK, width)
        tile_now = tile_dev[device].astype(jnp.float32)
        summed = jnp.einsum('bpij,bpjf->bif', tile_now, sources.astype(jnp.float32))
        deg_now = degree[device][:, None]
        mean_agg = (summed.reshape(rows_dev, width) / deg_now).astype(jnp.bfloat16)
        feature = feat_dev[device]
        preact = jnp.dot(feature, w_self, preferred_element_type=jnp.float32) + jnp.dot(mean_agg, w_neigh, preferred_element_type=jnp.float32) + bias
        sigma = jax.nn.sigmoid(preact)
        layer_out = (preact * sigma).astype(jnp.bfloat16)
        cot_now = cot_dev[device].astype(jnp.float32)
        grad_pre = (cot_now * sigma * (1.0 + preact * (1.0 - sigma))).astype(jnp.bfloat16)
        sum_self = sum_self + jnp.dot(feature.T, grad_pre, preferred_element_type=jnp.float32)
        sum_neigh = sum_neigh + jnp.dot(mean_agg.T, grad_pre, preferred_element_type=jnp.float32)
        sum_bias = sum_bias + lax.optimization_barrier(jnp.sum(grad_pre.astype(jnp.float32), axis=0))
        grad_mean = (jnp.dot(grad_pre, w_neigh.T, preferred_element_type=jnp.float32) / deg_now).astype(jnp.bfloat16)
        grad_mean = grad_mean.reshape(B_DEV, BLOCK, width)
        pair_grads = jnp.einsum('bpij,bif->bpjf', tile_now, grad_mean.astype(jnp.float32))
        pair_grads = pair_grads.reshape(B_DEV * P_SIZE, BLOCK, width)
        entry_grads = jnp.zeros((B_DEV + 2 + N_DOM, BLOCK, width), jnp.float32).at[pairs].add(pair_grads)
        slot_part = lax.optimization_barrier(entry_grads[B_DEV + 2:].astype(jnp.bfloat16)).astype(jnp.float32)
        entry_grads = jnp.concatenate([entry_grads[:B_DEV + 2], slot_part], axis=0)
        self_part = jnp.dot(grad_pre, w_self.T, preferred_element_type=jnp.float32).reshape(B_DEV, BLOCK, width)
        grad_sum = grad_sum.at[entry_ids].add(entry_grads)
        grad_sum = grad_sum.at[own_ids].add(self_part)
        return ((grad_sum, sum_self, sum_neigh, sum_bias), layer_out)
    start = (jnp.zeros((zero_id + 1, BLOCK, width), jnp.float32), jnp.zeros((width, hidden), jnp.float32), jnp.zeros((width, hidden), jnp.float32), jnp.zeros((hidden,), jnp.float32))
    final, outputs = lax.scan(step, start, jnp.arange(devices, dtype=jnp.int32))
    grad_sum, sum_self, sum_neigh, sum_bias = final
    grad_scale = 1.0 / jnp.sqrt(jnp.float32(NODES))
    layer_out = outputs.reshape(NODES, hidden)
    grad_features = grad_sum[:zero_id].reshape(NODES, width).astype(jnp.bfloat16)
    return (layer_out, grad_features, sum_self * grad_scale, sum_neigh * grad_scale, sum_bias * grad_scale)
```

```python
import math

import jax
import jax.numpy as jnp
from jax import lax
from jax.sharding import PartitionSpec as P


def with_halo(block, sides, width):
    for axis, dim in sides:
        count = lax.axis_size(axis)
        forward = [(i, i + 1) for i in range(count - 1)]
        backward = [(target, source) for source, target in forward]
        low = lax.ppermute(
            lax.slice_in_dim(block, block.shape[dim] - width, None, axis=dim), axis, forward
        )
        high = lax.ppermute(lax.slice_in_dim(block, 0, width, axis=dim), axis, backward)
        block = jnp.concatenate([low, block, high], axis=dim)
    return block


LANES = 128


def reduce_grads(local_self, local_neigh, local_bias, scale):
    dom_size = lax.axis_size("dom")
    inner_size = lax.axis_size("inner")
    width, hidden = local_self.shape
    both = jnp.concatenate([local_self, local_neigh], axis=0).astype(jnp.bfloat16)
    rows = both.size // (inner_size * LANES)
    chunks = both.reshape(inner_size, rows, LANES)
    pieces = lax.all_to_all(chunks, "inner", split_axis=0, concat_axis=0, tiled=True)
    piece = jnp.sum(pieces.astype(jnp.float32), axis=0)
    bias_rows = hidden // LANES
    spare = jnp.zeros((8 - bias_rows, LANES), jnp.float32)
    piece = jnp.concatenate([piece, local_bias.reshape(bias_rows, LANES), spare], axis=0)
    spread = jnp.broadcast_to(piece[None], (dom_size,) + piece.shape)
    spread = lax.all_to_all(spread, "dom", split_axis=0, concat_axis=0, tiled=True)
    piece = (jnp.sum(spread, axis=0) * scale).astype(jnp.bfloat16)
    spread = jnp.broadcast_to(piece[None], (inner_size,) + piece.shape)
    spread = lax.all_to_all(spread, "inner", split_axis=0, concat_axis=0, tiled=True)
    whole = spread[:, :rows].astype(jnp.float32).reshape(2, width, hidden)
    sum_bias = jnp.sum(spread[:, rows : rows + bias_rows].astype(jnp.float32), axis=0)
    return whole[0], whole[1], sum_bias.reshape(hidden)


def per_device(
    features, tiles, pair_source, in_degree, send_blocks, w_self, w_neigh, bias, cotangent
):
    rows_dev, width = features.shape
    nblocks = tiles.shape[0]
    npairs = tiles.shape[1]
    block_rows = tiles.shape[2]
    dom_size = lax.axis_size("dom")
    entries = nblocks + 2 + dom_size
    blocks = features.reshape(nblocks, block_rows, width)
    padded = with_halo(features, (("inner", 0),), block_rows)
    left_rim = padded[:block_rows]
    right_rim = padded[rows_dev + block_rows :]
    block_range = jnp.arange(nblocks, dtype=jnp.int32)
    chosen = (send_blocks[0][:, None] == block_range[None, :]).astype(jnp.bfloat16)
    outgoing = jnp.einsum("jb,brf->jrf", chosen, blocks, preferred_element_type=jnp.float32).astype(
        jnp.bfloat16
    )
    received = lax.all_to_all(outgoing, "dom", split_axis=0, concat_axis=0, tiled=True)
    source_table = jnp.concatenate([blocks, left_rim[None], right_rim[None], received], axis=0)
    flat_pairs = pair_source.reshape(nblocks * npairs)
    selector = flat_pairs[:, None] == jnp.arange(entries, dtype=jnp.int32)[None, :]
    sources = jnp.einsum(
        "nt,tjf->njf",
        selector.astype(jnp.bfloat16),
        source_table,
        preferred_element_type=jnp.float32,
    ).astype(jnp.bfloat16)
    sources = sources.reshape(nblocks, npairs, block_rows, width)
    summed = jnp.einsum("bpij,bpjf->bif", tiles, sources, preferred_element_type=jnp.float32)
    degree = in_degree.astype(jnp.float32)[:, None]
    mean_agg = (summed.reshape(rows_dev, width) / degree).astype(jnp.bfloat16)
    preact = (
        jnp.dot(features, w_self, preferred_element_type=jnp.float32)
        + jnp.dot(mean_agg, w_neigh, preferred_element_type=jnp.float32)
        + bias
    )
    sigma = jax.nn.sigmoid(preact)
    layer_out = (preact * sigma).astype(jnp.bfloat16)
    grad_pre = (cotangent.astype(jnp.float32) * sigma * (1.0 + preact * (1.0 - sigma))).astype(
        jnp.bfloat16
    )
    contract_rows = (((0,), (0,)), ((), ()))
    contract_cols = (((1,), (1,)), ((), ()))
    local_self = lax.dot_general(
        features, grad_pre, contract_rows, preferred_element_type=jnp.float32
    )
    local_neigh = lax.dot_general(
        mean_agg, grad_pre, contract_rows, preferred_element_type=jnp.float32
    )
    local_bias = jnp.sum(grad_pre.astype(jnp.float32), axis=0)
    grad_mean = (
        lax.dot_general(grad_pre, w_neigh, contract_cols, preferred_element_type=jnp.float32)
        / degree
    )
    grad_mean = grad_mean.astype(jnp.bfloat16).reshape(nblocks, block_rows, width)
    pair_grads = jnp.einsum("bpij,bif->bpjf", tiles, grad_mean, preferred_element_type=jnp.float32)
    pair_grads = pair_grads.reshape(nblocks * npairs, block_rows, width)
    entry_grads = jax.ops.segment_sum(pair_grads, flat_pairs, num_segments=entries)
    rim_grads = jnp.concatenate([entry_grads[nblocks], entry_grads[nblocks + 1]], axis=0)
    returned_rims = with_halo(rim_grads.astype(jnp.bfloat16), (("inner", 0),), block_rows).astype(
        rim_grads.dtype
    )
    slot_grads = entry_grads[nblocks + 2 :].astype(jnp.bfloat16)
    returned = lax.all_to_all(slot_grads, "dom", split_axis=0, concat_axis=0, tiled=True)
    sent_map = (send_blocks[0][:, None] == block_range[None, :]).astype(jnp.bfloat16)
    returned_sum = jnp.einsum("jb,jrf->brf", sent_map, returned, preferred_element_type=jnp.float32)
    self_part = lax.dot_general(grad_pre, w_self, contract_cols, preferred_element_type=jnp.float32)
    total = self_part.reshape(nblocks, block_rows, width) + entry_grads[:nblocks] + returned_sum
    total = total.at[0].add(returned_rims[:block_rows])
    total = total.at[nblocks - 1].add(returned_rims[3 * block_rows :])
    grad_scale = 1.0 / math.sqrt(rows_dev * dom_size * lax.axis_size("inner"))
    sum_self, sum_neigh, sum_bias = reduce_grads(local_self, local_neigh, local_bias, grad_scale)
    grad_features = total.reshape(rows_dev, width).astype(jnp.bfloat16)
    return (
        layer_out,
        grad_features,
        sum_self,
        sum_neigh,
        sum_bias,
    )


def solution(mesh):
    return jax.shard_map(
        per_device,
        mesh=mesh,
        in_specs=(
            P(("dom", "inner"), None),
            P(("dom", "inner"), None, None, None),
            P(("dom", "inner"), None),
            P(("dom", "inner")),
            P(("dom", "inner"), None),
            P(),
            P(),
            P(),
            P(("dom", "inner"), None),
        ),
        out_specs=(P(("dom", "inner"), None), P(("dom", "inner"), None), P(), P(), P()),
        check_vma=False,
    )
```

```python
import functools
import math

import jax
import jax.numpy as jnp
from jax import lax
from jax.experimental import pallas as pl
from jax.experimental.pallas import tpu as pltpu
from jax.sharding import PartitionSpec as P

LANES = 128
VMEM = pl.BlockSpec(memory_space=pltpu.VMEM)
SMEM = pl.BlockSpec(memory_space=pltpu.SMEM)
ANY = pl.BlockSpec(memory_space=pl.ANY)
F32 = jnp.float32
BF16 = jnp.bfloat16
CONTRACT_ROWS = (((0,), (0,)), ((), ()))
CONTRACT_COLS = (((1,), (1,)), ((), ()))


def params():
    return pltpu.CompilerParams(vmem_limit_bytes=32 * 1024 * 1024)


def pick_kernel(send_ref, blocks_ref, out_ref, sems):
    copies = []
    for j in range(out_ref.shape[0]):
        copies.append(
            pltpu.make_async_copy(blocks_ref.at[send_ref[0, j]], out_ref.at[j], sems.at[j])
        )
    for copy in copies:
        copy.start()
    for copy in copies:
        copy.wait()


def layer_kernel(
    pairs_ref,
    degree_ref,
    w_self_ref,
    w_neigh_ref,
    bias_ref,
    blocks_hbm,
    left_hbm,
    right_hbm,
    received_hbm,
    tiles_hbm,
    cot_hbm,
    out_hbm,
    own_ref,
    rims_ref,
    slots_ref,
    grads_ref,
    gbias_ref,
    table,
    tiles,
    cot,
    out,
    sources,
    mean,
    grad_pre,
    inverse,
    entries,
    sems,
    tile_sems,
):
    nblocks, npairs, rows, _ = tiles.shape
    width = table.shape[2]
    copies = [
        pltpu.make_async_copy(blocks_hbm, table.at[pl.ds(0, nblocks)], sems.at[0]),
        pltpu.make_async_copy(left_hbm, table.at[nblocks], sems.at[1]),
        pltpu.make_async_copy(right_hbm, table.at[nblocks + 1], sems.at[2]),
        pltpu.make_async_copy(
            received_hbm, table.at[pl.ds(nblocks + 2, received_hbm.shape[0])], sems.at[3]
        ),
    ]
    tile_copies = [
        pltpu.make_async_copy(tiles_hbm.at[b], tiles.at[b], tile_sems.at[b])
        for b in range(nblocks)
    ]
    cot_copy = pltpu.make_async_copy(cot_hbm, cot, sems.at[4])
    out_copy = pltpu.make_async_copy(out, out_hbm, sems.at[5])
    for copy in copies:
        copy.start()
    for copy in tile_copies:
        copy.start()
    cot_copy.start()

    for b in range(nblocks):
        row = 1.0 / degree_ref[b : b + 1, :].astype(F32)
        inverse[b] = jnp.broadcast_to(row, (rows, rows)).T
    entries[nblocks:] = jnp.zeros((entries.shape[0] - nblocks, rows, width), F32)

    for copy in copies:
        copy.wait()

    def tile_row(b):
        return jnp.concatenate([tiles[b, p] for p in range(npairs)], axis=1)

    def by_degree(values, b):
        return jnp.concatenate(
            [values[:, k : k + rows] * inverse[b] for k in range(0, width, rows)], axis=1
        )

    for b in range(nblocks):
        for p in range(npairs):
            sources[b % 2, pl.ds(p * rows, rows), :] = table[pairs_ref[b, p]]
        tile_copies[b].wait()
        summed = jnp.dot(tile_row(b), sources[b % 2], preferred_element_type=F32)
        mean[b] = by_degree(summed, b).astype(BF16)

    cot_copy.wait()
    w_self = w_self_ref[...]
    w_neigh = w_neigh_ref[...]
    gbias = jnp.zeros((1, width), F32)
    step = 2
    for b in range(0, nblocks, step):
        features = table[b : b + step].reshape(step * rows, width)
        means = mean[b : b + step].reshape(step * rows, width)
        preact = (
            jnp.dot(features, w_self, preferred_element_type=F32)
            + jnp.dot(means, w_neigh, preferred_element_type=F32)
            + bias_ref[...]
        )
        sigma = jax.nn.sigmoid(preact)
        out[b : b + step] = (preact * sigma).astype(BF16).reshape(step, rows, width)
        cots = cot[b : b + step].reshape(step * rows, width).astype(F32)
        grad = (cots * sigma * (1.0 + preact * (1.0 - sigma))).astype(BF16)
        grad_pre[pl.ds(b * rows, step * rows), :] = grad
        gbias = gbias + jnp.sum(grad.astype(F32), axis=0, keepdims=True)
        own = lax.dot_general(grad, w_self, CONTRACT_COLS, preferred_element_type=F32)
        entries[b : b + step] = own.reshape(step, rows, width)
    out_copy.start()
    gbias_ref[...] = gbias

    for b in range(nblocks):
        grad = grad_pre[pl.ds(b * rows, rows), :]
        grad_mean = lax.dot_general(grad, w_neigh, CONTRACT_COLS, preferred_element_type=F32)
        grad_mean = by_degree(grad_mean, b).astype(BF16)
        parts = lax.dot_general(
            tile_row(b), grad_mean, CONTRACT_ROWS, preferred_element_type=F32
        )
        for p in range(npairs):
            entry = pairs_ref[b, p]
            entries[entry] = entries[entry] + parts[p * rows : (p + 1) * rows]

    own_ref[...] = entries[:nblocks]
    rims_ref[...] = entries[nblocks : nblocks + 2].astype(BF16)
    slots_ref[...] = entries[nblocks + 2 :].astype(BF16)

    grads = grad_pre[...]
    features = table[:nblocks].reshape(nblocks * rows, width)
    means = mean[...].reshape(nblocks * rows, width)
    grads_ref[:width, :] = lax.dot_general(
        features, grads, CONTRACT_ROWS, preferred_element_type=F32
    ).astype(BF16)
    grads_ref[width:, :] = lax.dot_general(
        means, grads, CONTRACT_ROWS, preferred_element_type=F32
    ).astype(BF16)
    out_copy.wait()


def combine_kernel(send_ref, own_ref, returned_ref, low_ref, high_ref, out_ref, total):
    total[...] = own_ref[...]
    last = total.shape[0] - 1
    total[0] = total[0] + low_ref[...].astype(F32)
    total[last] = total[last] + high_ref[...].astype(F32)
    for j in range(returned_ref.shape[0]):
        block = send_ref[0, j]
        total[block] = total[block] + returned_ref[j].astype(F32)
    out_ref[...] = total[...].astype(BF16)


def call_layer(
    blocks, left, right, received, tiles, cot, pairs, degree, w_self, w_neigh, bias
):
    nblocks, npairs, rows, _ = tiles.shape
    width = blocks.shape[2]
    dom = received.shape[0]
    entries = nblocks + 2 + dom
    shape = jax.ShapeDtypeStruct
    return pl.pallas_call(
        layer_kernel,
        out_shape=(
            shape(blocks.shape, BF16),
            shape(blocks.shape, F32),
            shape((2, rows, width), BF16),
            shape((dom, rows, width), BF16),
            shape((2 * width, width), BF16),
            shape((1, width), F32),
        ),
        in_specs=[SMEM] + [VMEM] * 4 + [ANY] * 6,
        out_specs=(ANY,) + (VMEM,) * 5,
        scratch_shapes=[
            pltpu.VMEM((entries, rows, width), BF16),
            pltpu.VMEM(tiles.shape, BF16),
            pltpu.VMEM(blocks.shape, BF16),
            pltpu.VMEM(blocks.shape, BF16),
            pltpu.VMEM((2, npairs * rows, width), BF16),
            pltpu.VMEM(blocks.shape, BF16),
            pltpu.VMEM((nblocks * rows, width), BF16),
            pltpu.VMEM((nblocks, rows, rows), F32),
            pltpu.VMEM((entries, rows, width), F32),
            pltpu.SemaphoreType.DMA((6,)),
            pltpu.SemaphoreType.DMA((nblocks,)),
        ],
        compiler_params=params(),
        cost_estimate=pl.CostEstimate(
            flops=4 * 10**9, bytes_accessed=8 * 10**6, transcendentals=nblocks * rows * width
        ),
    )(pairs, degree, w_self, w_neigh, bias, blocks, left, right, received, tiles, cot)


def neighbours(low_source, high_source, axis):
    count = lax.axis_size(axis)
    forward = [(i, i + 1) for i in range(count - 1)]
    backward = [(target, source) for source, target in forward]
    return lax.ppermute(low_source, axis, forward), lax.ppermute(high_source, axis, backward)


def reduce_grads(grads, gbias, scale):
    dom_size = lax.axis_size("dom")
    inner_size = lax.axis_size("inner")
    hidden = grads.shape[1]
    rows = grads.shape[0] // inner_size
    chunks = grads.reshape(inner_size, rows, hidden)
    pieces = lax.all_to_all(chunks, "inner", split_axis=0, concat_axis=0, tiled=True)
    piece = jnp.sum(pieces.astype(F32), axis=0)
    piece = [piece[:, k : k + LANES] for k in range(0, hidden, LANES)]
    bias_rows = hidden // LANES
    spare = jnp.zeros((8 - bias_rows, LANES), F32)
    piece = jnp.concatenate(piece + [gbias.reshape(bias_rows, LANES), spare], axis=0)
    spread = jnp.broadcast_to(piece[None], (dom_size,) + piece.shape)
    spread = lax.all_to_all(spread, "dom", split_axis=0, concat_axis=0, tiled=True)
    piece = (jnp.sum(spread, axis=0) * scale).astype(BF16)
    spread = jnp.broadcast_to(piece[None], (inner_size,) + piece.shape)
    spread = lax.all_to_all(spread, "inner", split_axis=0, concat_axis=0, tiled=True)
    return pl.pallas_call(
        functools.partial(unpack_kernel, rows, bias_rows),
        out_shape=(
            jax.ShapeDtypeStruct((hidden, hidden), F32),
            jax.ShapeDtypeStruct((hidden, hidden), F32),
            jax.ShapeDtypeStruct((bias_rows, LANES), F32),
        ),
        in_specs=[VMEM],
        out_specs=(VMEM,) * 3,
        compiler_params=params(),
    )(spread)


def unpack_kernel(rows, bias_rows, spread_ref, self_ref, neigh_ref, bias_ref):
    spread = spread_ref[...].astype(F32)
    half = spread.shape[0] // 2
    for k in range(bias_rows):
        part = spread[:, k * rows : (k + 1) * rows]
        for ref, first in ((self_ref, 0), (neigh_ref, half)):
            ref[:, k * LANES : (k + 1) * LANES] = part[first : first + half].reshape(-1, LANES)
    tail = jnp.sum(spread[:, bias_rows * rows :], axis=0)
    bias_ref[...] = tail[:bias_rows]


def per_device(
    features, tiles, pair_source, in_degree, send_blocks, w_self, w_neigh, bias, cotangent
):
    rows_dev, width = features.shape
    nblocks, _, rows, _ = tiles.shape
    dom_size = lax.axis_size("dom")
    blocks = features.reshape(nblocks, rows, width)
    outgoing = pl.pallas_call(
        pick_kernel,
        out_shape=jax.ShapeDtypeStruct((dom_size, rows, width), BF16),
        in_specs=[SMEM, ANY],
        out_specs=ANY,
        scratch_shapes=[pltpu.SemaphoreType.DMA((dom_size,))],
    )(send_blocks, blocks)
    received = lax.all_to_all(outgoing, "dom", split_axis=0, concat_axis=0, tiled=True)
    left, right = neighbours(blocks[nblocks - 1], blocks[0], "inner")
    layer_out, own, rims, slots, grads, gbias = call_layer(
        blocks,
        left,
        right,
        received,
        tiles,
        cotangent.reshape(nblocks, rows, width),
        pair_source,
        in_degree.reshape(nblocks, rows),
        w_self,
        w_neigh,
        bias[None, :],
    )
    returned = lax.all_to_all(slots, "dom", split_axis=0, concat_axis=0, tiled=True)
    low, high = neighbours(rims[1], rims[0], "inner")
    grad_features = pl.pallas_call(
        combine_kernel,
        out_shape=jax.ShapeDtypeStruct(blocks.shape, BF16),
        in_specs=[SMEM] + [VMEM] * 4,
        out_specs=VMEM,
        scratch_shapes=[pltpu.VMEM(blocks.shape, F32)],
        compiler_params=params(),
        cost_estimate=pl.CostEstimate(
            flops=10**6, bytes_accessed=3 * 10**6, transcendentals=0
        ),
    )(send_blocks, own, returned, low, high)
    scale = 1.0 / math.sqrt(rows_dev * dom_size * lax.axis_size("inner"))
    sum_self, sum_neigh, sum_bias = reduce_grads(grads, gbias, scale)
    return (
        layer_out.reshape(rows_dev, width),
        grad_features.reshape(rows_dev, width),
        sum_self,
        sum_neigh,
        sum_bias.reshape(-1),
    )


def solution(mesh):
    return jax.shard_map(
        per_device,
        mesh=mesh,
        in_specs=(
            P(("dom", "inner"), None),
            P(("dom", "inner"), None, None, None),
            P(("dom", "inner"), None),
            P(("dom", "inner")),
            P(("dom", "inner"), None),
            P(),
            P(),
            P(),
            P(("dom", "inner"), None),
        ),
        out_specs=(P(("dom", "inner"), None), P(("dom", "inner"), None), P(), P(), P()),
        check_vma=False,
    )
```

```python
import functools
import math

import jax
import jax.numpy as jnp
from jax import lax
from jax.experimental import pallas as pl
from jax.experimental.pallas import tpu as pltpu
from jax.sharding import PartitionSpec as P

LANES = 128
VMEM = pl.BlockSpec(memory_space=pltpu.VMEM)
SMEM = pl.BlockSpec(memory_space=pltpu.SMEM)
ANY = pl.BlockSpec(memory_space=pl.ANY)
HBM = pl.BlockSpec(memory_space=pltpu.HBM)
F32 = jnp.float32
BF16 = jnp.bfloat16
CONTRACT_ROWS = (((0,), (0,)), ((), ()))
CONTRACT_COLS = (((1,), (1,)), ((), ()))


def params():
    return pltpu.CompilerParams(vmem_limit_bytes=32 * 1024 * 1024)


def pick_kernel(send_ref, blocks_ref, out_ref):
    for j in range(out_ref.shape[0]):
        out_ref[j] = blocks_ref[send_ref[0, j]]


def merge_kernel(pieces_ref, gbias_ref, slots_ref, merged_ref, piece, sems):
    rows = slots_ref.shape[1] - piece.shape[0]
    summed = jnp.sum(pieces_ref[...].astype(F32), axis=0)
    bias = gbias_ref[...]
    high = bias.astype(BF16).astype(F32)
    tail = jnp.concatenate(
        [high, bias - high, jnp.zeros((6, bias.shape[1]), F32)], axis=0
    )
    piece[...] = jnp.concatenate([summed, tail], axis=0).astype(BF16)
    copies = [
        pltpu.make_async_copy(
            piece, merged_ref.at[j, pl.ds(rows, piece.shape[0])], sems.at[j]
        )
        for j in range(merged_ref.shape[0])
    ]
    for copy in copies:
        copy.start()
    for copy in copies:
        copy.wait()


def layer_kernel(
    pairs_ref,
    degree_ref,
    w_self_ref,
    w_neigh_ref,
    bias_ref,
    blocks_hbm,
    left_hbm,
    right_hbm,
    received_hbm,
    tiles_hbm,
    cot_hbm,
    out_hbm,
    own_ref,
    rims_ref,
    slots_ref,
    grads_ref,
    gbias_ref,
    table,
    tiles,
    cot,
    out,
    sources,
    mean,
    grad_pre,
    inverse,
    entries,
    sems,
    tile_sems,
):
    nblocks, npairs, rows, _ = tiles.shape
    width = table.shape[2]
    copies = [
        pltpu.make_async_copy(blocks_hbm, table.at[pl.ds(0, nblocks)], sems.at[0]),
        pltpu.make_async_copy(left_hbm, table.at[nblocks], sems.at[1]),
        pltpu.make_async_copy(right_hbm, table.at[nblocks + 1], sems.at[2]),
        pltpu.make_async_copy(
            received_hbm, table.at[pl.ds(nblocks + 2, received_hbm.shape[0])], sems.at[3]
        ),
    ]
    tile_copies = [
        pltpu.make_async_copy(tiles_hbm.at[b], tiles.at[b], tile_sems.at[b])
        for b in range(nblocks)
    ]
    cot_copy = pltpu.make_async_copy(cot_hbm, cot, sems.at[4])
    out_copy = pltpu.make_async_copy(out, out_hbm, sems.at[5])
    for copy in copies:
        copy.start()
    for copy in tile_copies:
        copy.start()
    cot_copy.start()

    for b in range(nblocks):
        row = 1.0 / degree_ref[b : b + 1, :].astype(F32)
        inverse[b] = jnp.broadcast_to(row, (rows, rows)).T
    entries[nblocks:] = jnp.zeros((entries.shape[0] - nblocks, rows, width), F32)

    for copy in copies:
        copy.wait()

    def tile_row(b):
        return jnp.concatenate([tiles[b, p] for p in range(npairs)], axis=1)

    def by_degree(values, b):
        return jnp.concatenate(
            [values[:, k : k + rows] * inverse[b] for k in range(0, width, rows)], axis=1
        )

    for b in range(nblocks):
        for p in range(npairs):
            sources[b % 2, pl.ds(p * rows, rows), :] = table[pairs_ref[b, p]]
        tile_copies[b].wait()
        summed = jnp.dot(tile_row(b), sources[b % 2], preferred_element_type=F32)
        mean[b] = by_degree(summed, b).astype(BF16)

    cot_copy.wait()
    w_self = w_self_ref[...]
    w_neigh = w_neigh_ref[...]
    gbias = jnp.zeros((1, width), F32)
    step = 2
    for b in range(0, nblocks, step):
        features = table[b : b + step].reshape(step * rows, width)
        means = mean[b : b + step].reshape(step * rows, width)
        preact = (
            jnp.dot(features, w_self, preferred_element_type=F32)
            + jnp.dot(means, w_neigh, preferred_element_type=F32)
            + bias_ref[...]
        )
        sigma = jax.nn.sigmoid(preact)
        out[b : b + step] = (preact * sigma).astype(BF16).reshape(step, rows, width)
        cots = cot[b : b + step].reshape(step * rows, width).astype(F32)
        grad = (cots * sigma * (1.0 + preact * (1.0 - sigma))).astype(BF16)
        grad_pre[pl.ds(b * rows, step * rows), :] = grad
        gbias = gbias + jnp.sum(grad.astype(F32), axis=0, keepdims=True)
        own = lax.dot_general(grad, w_self, CONTRACT_COLS, preferred_element_type=F32)
        entries[b : b + step] = own.reshape(step, rows, width)
    out_copy.start()
    gbias_ref[...] = gbias

    for b in range(nblocks):
        grad = grad_pre[pl.ds(b * rows, rows), :]
        grad_mean = lax.dot_general(grad, w_neigh, CONTRACT_COLS, preferred_element_type=F32)
        grad_mean = by_degree(grad_mean, b).astype(BF16)
        parts = lax.dot_general(
            tile_row(b), grad_mean, CONTRACT_ROWS, preferred_element_type=F32
        )
        for p in range(npairs):
            entry = pairs_ref[b, p]
            entries[entry] = entries[entry] + parts[p * rows : (p + 1) * rows]

    own_ref[...] = entries[:nblocks]
    rims_ref[...] = entries[nblocks : nblocks + 2].astype(BF16)
    slots_ref[:, :rows, :] = entries[nblocks + 2 :].astype(BF16)
    slots_ref[:, rows:, :] = jnp.zeros(
        (slots_ref.shape[0], slots_ref.shape[1] - rows, width), BF16
    )

    grads = grad_pre[...]
    features = table[:nblocks].reshape(nblocks * rows, width)
    means = mean[...].reshape(nblocks * rows, width)
    grads_ref[:width, :] = lax.dot_general(
        features, grads, CONTRACT_ROWS, preferred_element_type=F32
    ).astype(BF16)
    grads_ref[width:, :] = lax.dot_general(
        means, grads, CONTRACT_ROWS, preferred_element_type=F32
    ).astype(BF16)
    out_copy.wait()


def combine_kernel(send_ref, own_ref, returned_ref, low_ref, high_ref, out_ref, total):
    total[...] = own_ref[...]
    last = total.shape[0] - 1
    total[0] = total[0] + low_ref[...].astype(F32)
    total[last] = total[last] + high_ref[...].astype(F32)
    for j in range(returned_ref.shape[0]):
        block = send_ref[0, j]
        total[block] = total[block] + returned_ref[j, : total.shape[1]].astype(F32)
    out_ref[...] = total[...].astype(BF16)


def call_layer(
    blocks, left, right, received, tiles, cot, pairs, degree, w_self, w_neigh, bias
):
    nblocks, npairs, rows, _ = tiles.shape
    width = blocks.shape[2]
    dom = received.shape[0]
    entries = nblocks + 2 + dom
    extra = 2 * width // lax.axis_size("inner") + 8
    shape = jax.ShapeDtypeStruct
    return pl.pallas_call(
        layer_kernel,
        out_shape=(
            shape(blocks.shape, BF16),
            shape(blocks.shape, F32),
            shape((2, rows, width), BF16),
            shape((dom, rows + extra, width), BF16),
            shape((2 * width, width), BF16),
            shape((1, width), F32),
        ),
        in_specs=[SMEM] + [VMEM] * 4 + [ANY] * 4 + [HBM] * 2,
        out_specs=(ANY,) + (VMEM,) * 5,
        scratch_shapes=[
            pltpu.VMEM((entries, rows, width), BF16),
            pltpu.VMEM(tiles.shape, BF16),
            pltpu.VMEM(blocks.shape, BF16),
            pltpu.VMEM(blocks.shape, BF16),
            pltpu.VMEM((2, npairs * rows, width), BF16),
            pltpu.VMEM(blocks.shape, BF16),
            pltpu.VMEM((nblocks * rows, width), BF16),
            pltpu.VMEM((nblocks, rows, rows), F32),
            pltpu.VMEM((entries, rows, width), F32),
            pltpu.SemaphoreType.DMA((6,)),
            pltpu.SemaphoreType.DMA((nblocks,)),
        ],
        compiler_params=params(),
        cost_estimate=pl.CostEstimate(
            flops=4 * 10**9, bytes_accessed=8 * 10**6, transcendentals=nblocks * rows * width
        ),
    )(pairs, degree, w_self, w_neigh, bias, blocks, left, right, received, tiles, cot)


def neighbours(low_source, high_source, axis):
    count = lax.axis_size(axis)
    forward = [(i, i + 1) for i in range(count - 1)]
    backward = [(target, source) for source, target in forward]
    return lax.ppermute(low_source, axis, forward), lax.ppermute(high_source, axis, backward)


def merge_grads(grads, gbias, slots):
    inner_size = lax.axis_size("inner")
    hidden = grads.shape[1]
    chunks = grads.reshape(inner_size, grads.shape[0] // inner_size, hidden)
    pieces = lax.all_to_all(chunks, "inner", split_axis=0, concat_axis=0, tiled=True)
    return pl.pallas_call(
        merge_kernel,
        out_shape=jax.ShapeDtypeStruct(slots.shape, BF16),
        in_specs=[VMEM, VMEM, ANY],
        out_specs=ANY,
        scratch_shapes=[
            pltpu.VMEM((chunks.shape[1] + 8, hidden), BF16),
            pltpu.SemaphoreType.DMA((slots.shape[0],)),
        ],
        input_output_aliases={2: 0},
        compiler_params=params(),
    )(pieces, gbias, slots)


def spread_grads(extra, scale):
    inner_size = lax.axis_size("inner")
    hidden = extra.shape[2]
    rows = extra.shape[1] - 8
    summed = jnp.sum(extra.astype(F32), axis=0) * scale
    lanes = [summed[:rows, k : k + LANES] for k in range(0, hidden, LANES)]
    bias = (summed[rows] + summed[rows + 1]).reshape(-1, LANES)
    bias_rows = bias.shape[0]
    spare = jnp.zeros((8 - bias_rows, LANES), F32)
    piece = jnp.concatenate(lanes + [bias, spare], axis=0).astype(BF16)
    spread = jnp.broadcast_to(piece[None], (inner_size,) + piece.shape)
    spread = lax.all_to_all(spread, "inner", split_axis=0, concat_axis=0, tiled=True)
    return pl.pallas_call(
        functools.partial(unpack_kernel, rows, bias_rows),
        out_shape=(
            jax.ShapeDtypeStruct((hidden, hidden), F32),
            jax.ShapeDtypeStruct((hidden, hidden), F32),
            jax.ShapeDtypeStruct((bias_rows, LANES), F32),
        ),
        in_specs=[VMEM],
        out_specs=(VMEM,) * 3,
        compiler_params=params(),
    )(spread)


def unpack_kernel(rows, bias_rows, spread_ref, self_ref, neigh_ref, bias_ref):
    spread = spread_ref[...].astype(F32)
    half = spread.shape[0] // 2
    for k in range(bias_rows):
        part = spread[:, k * rows : (k + 1) * rows]
        for ref, first in ((self_ref, 0), (neigh_ref, half)):
            ref[:, k * LANES : (k + 1) * LANES] = part[first : first + half].reshape(-1, LANES)
    tail = jnp.sum(spread[:, bias_rows * rows :], axis=0)
    bias_ref[...] = tail[:bias_rows]


def per_device(
    features, tiles, pair_source, in_degree, send_blocks, w_self, w_neigh, bias, cotangent
):
    rows_dev, width = features.shape
    nblocks, _, rows, _ = tiles.shape
    dom_size = lax.axis_size("dom")
    blocks = features.reshape(nblocks, rows, width)
    outgoing = pl.pallas_call(
        pick_kernel,
        out_shape=jax.ShapeDtypeStruct((dom_size, rows, width), BF16),
        in_specs=[SMEM, VMEM],
        out_specs=VMEM,
        compiler_params=params(),
    )(send_blocks, blocks)
    received = lax.all_to_all(outgoing, "dom", split_axis=0, concat_axis=0, tiled=True)
    left, right = neighbours(blocks[nblocks - 1], blocks[0], "inner")
    layer_out, own, rims, slots, grads, gbias = call_layer(
        blocks,
        left,
        right,
        received,
        tiles,
        cotangent.reshape(nblocks, rows, width),
        pair_source,
        in_degree.reshape(nblocks, rows),
        w_self,
        w_neigh,
        bias[None, :],
    )
    merged = merge_grads(grads, gbias, slots)
    returned = lax.all_to_all(merged, "dom", split_axis=0, concat_axis=0, tiled=True)
    low, high = neighbours(rims[1], rims[0], "inner")
    grad_features = pl.pallas_call(
        combine_kernel,
        out_shape=jax.ShapeDtypeStruct(blocks.shape, BF16),
        in_specs=[SMEM] + [VMEM] * 4,
        out_specs=VMEM,
        scratch_shapes=[pltpu.VMEM(blocks.shape, F32)],
        compiler_params=params(),
        cost_estimate=pl.CostEstimate(
            flops=10**6, bytes_accessed=3 * 10**6, transcendentals=0
        ),
    )(send_blocks, own, returned, low, high)
    scale = 1.0 / math.sqrt(rows_dev * dom_size * lax.axis_size("inner"))
    sum_self, sum_neigh, sum_bias = spread_grads(returned[:, rows:], scale)
    return (
        layer_out.reshape(rows_dev, width),
        grad_features.reshape(rows_dev, width),
        sum_self,
        sum_neigh,
        sum_bias.reshape(-1),
    )


def solution(mesh):
    return jax.shard_map(
        per_device,
        mesh=mesh,
        in_specs=(
            P(("dom", "inner"), None),
            P(("dom", "inner"), None, None, None),
            P(("dom", "inner"), None),
            P(("dom", "inner")),
            P(("dom", "inner"), None),
            P(),
            P(),
            P(),
            P(("dom", "inner"), None),
        ),
        out_specs=(P(("dom", "inner"), None), P(("dom", "inner"), None), P(), P(), P()),
        check_vma=False,
    )
```

```python
import functools
import math

import jax
import jax.numpy as jnp
from jax import lax
from jax.experimental import pallas as pl
from jax.experimental.pallas import tpu as pltpu
from jax.sharding import PartitionSpec as P

LANES = 128
VMEM = pl.BlockSpec(memory_space=pltpu.VMEM)
SMEM = pl.BlockSpec(memory_space=pltpu.SMEM)
ANY = pl.BlockSpec(memory_space=pl.ANY)
HBM = pl.BlockSpec(memory_space=pltpu.HBM)
F32 = jnp.float32
BF16 = jnp.bfloat16
CONTRACT_ROWS = (((0,), (0,)), ((), ()))
CONTRACT_COLS = (((1,), (1,)), ((), ()))


def params(mebibytes=32):
    return pltpu.CompilerParams(vmem_limit_bytes=mebibytes * 1024 * 1024)


def pick_kernel(send_ref, blocks_ref, out_ref, sems):
    copies = [
        pltpu.make_async_copy(blocks_ref.at[send_ref[0, j]], out_ref.at[j], sems.at[j])
        for j in range(out_ref.shape[0])
    ]
    for copy in copies:
        copy.start()
    for copy in copies:
        copy.wait()


def merge_kernel(pieces_ref, gbias_ref, slots_ref, merged_ref, piece, sems):
    rows = slots_ref.shape[1] - piece.shape[0]
    summed = jnp.sum(pieces_ref[...].astype(F32), axis=0)
    bias = gbias_ref[...]
    high = bias.astype(BF16).astype(F32)
    tail = jnp.concatenate(
        [high, bias - high, jnp.zeros((6, bias.shape[1]), F32)], axis=0
    )
    piece[...] = jnp.concatenate([summed, tail], axis=0).astype(BF16)
    copies = [
        pltpu.make_async_copy(
            piece, merged_ref.at[j, pl.ds(rows, piece.shape[0])], sems.at[j]
        )
        for j in range(merged_ref.shape[0])
    ]
    for copy in copies:
        copy.start()
    for copy in copies:
        copy.wait()


def tile_row(tiles, b):
    return jnp.concatenate([tiles[b, p] for p in range(tiles.shape[1])], axis=1)


def by_degree(values, inverse, b):
    rows = inverse.shape[1]
    return jnp.concatenate(
        [values[:, k : k + rows] * inverse[b] for k in range(0, values.shape[1], rows)], axis=1
    )


def invert_degree(degree_ref, inverse):
    for b in range(inverse.shape[0]):
        row = 1.0 / degree_ref[b : b + 1, :].astype(F32)
        inverse[b] = jnp.broadcast_to(row, inverse.shape[1:]).T


def forward_kernel(
    pairs_ref,
    degree_ref,
    w_self_ref,
    w_neigh_ref,
    bias_ref,
    blocks_hbm,
    left_hbm,
    right_hbm,
    received_hbm,
    tiles_hbm,
    cot_hbm,
    out_hbm,
    grad_hbm,
    grads_ref,
    gbias_ref,
    table,
    tiles,
    cot,
    out,
    sources,
    mean,
    grad_pre,
    inverse,
    sems,
    tile_sems,
):
    nblocks, npairs, rows, _ = tiles.shape
    width = table.shape[2]
    copies = [
        pltpu.make_async_copy(blocks_hbm, table.at[pl.ds(0, nblocks)], sems.at[0]),
        pltpu.make_async_copy(left_hbm, table.at[nblocks], sems.at[1]),
        pltpu.make_async_copy(right_hbm, table.at[nblocks + 1], sems.at[2]),
        pltpu.make_async_copy(
            received_hbm, table.at[pl.ds(nblocks + 2, received_hbm.shape[0])], sems.at[3]
        ),
    ]
    tile_copies = [
        pltpu.make_async_copy(tiles_hbm.at[b], tiles.at[b], tile_sems.at[b])
        for b in range(nblocks)
    ]
    cot_copy = pltpu.make_async_copy(cot_hbm, cot, sems.at[4])
    out_copy = pltpu.make_async_copy(out, out_hbm, sems.at[5])
    grad_copy = pltpu.make_async_copy(grad_pre, grad_hbm, sems.at[6])
    for copy in copies:
        copy.start()
    for copy in tile_copies:
        copy.start()
    cot_copy.start()
    invert_degree(degree_ref, inverse)
    for copy in copies:
        copy.wait()

    for b in range(nblocks):
        for p in range(npairs):
            sources[b % 2, pl.ds(p * rows, rows), :] = table[pairs_ref[b, p]]
        tile_copies[b].wait()
        summed = jnp.dot(tile_row(tiles, b), sources[b % 2], preferred_element_type=F32)
        mean[b] = by_degree(summed, inverse, b).astype(BF16)

    cot_copy.wait()
    w_self = w_self_ref[...]
    w_neigh = w_neigh_ref[...]
    gbias = jnp.zeros((1, width), F32)
    step = 2
    for b in range(0, nblocks, step):
        features = table[b : b + step].reshape(step * rows, width)
        means = mean[b : b + step].reshape(step * rows, width)
        preact = (
            jnp.dot(features, w_self, preferred_element_type=F32)
            + jnp.dot(means, w_neigh, preferred_element_type=F32)
            + bias_ref[...]
        )
        sigma = jax.nn.sigmoid(preact)
        out[b : b + step] = (preact * sigma).astype(BF16).reshape(step, rows, width)
        cots = cot[b : b + step].reshape(step * rows, width).astype(F32)
        grad = (cots * sigma * (1.0 + preact * (1.0 - sigma))).astype(BF16)
        grad_pre[pl.ds(b * rows, step * rows), :] = grad
        gbias = gbias + jnp.sum(grad.astype(F32), axis=0, keepdims=True)
    grad_copy.start()
    out_copy.start()
    gbias_ref[...] = gbias

    grads = grad_pre[...]
    features = table[:nblocks].reshape(nblocks * rows, width)
    means = mean[...].reshape(nblocks * rows, width)
    grads_ref[:width, :] = lax.dot_general(
        features, grads, CONTRACT_ROWS, preferred_element_type=F32
    ).astype(BF16)
    grads_ref[width:, :] = lax.dot_general(
        means, grads, CONTRACT_ROWS, preferred_element_type=F32
    ).astype(BF16)
    grad_copy.wait()
    out_copy.wait()


def backward_kernel(
    pairs_ref,
    degree_ref,
    w_self_ref,
    w_neigh_ref,
    grad_ref,
    tiles_hbm,
    own_ref,
    rims_ref,
    slots_ref,
    tiles,
    inverse,
    entries,
    tile_sems,
):
    nblocks, npairs, rows, _ = tiles.shape
    width = w_self_ref.shape[0]
    tile_copies = [
        pltpu.make_async_copy(tiles_hbm.at[b], tiles.at[b], tile_sems.at[b])
        for b in range(nblocks)
    ]
    for copy in tile_copies:
        copy.start()
    invert_degree(degree_ref, inverse)
    entries[nblocks:] = jnp.zeros((entries.shape[0] - nblocks, rows, width), F32)
    w_self = w_self_ref[...]
    w_neigh = w_neigh_ref[...]
    own = lax.dot_general(grad_ref[...], w_self, CONTRACT_COLS, preferred_element_type=F32)
    entries[:nblocks] = own.reshape(nblocks, rows, width)
    for b in range(nblocks):
        grad = grad_ref[pl.ds(b * rows, rows), :]
        grad_mean = lax.dot_general(grad, w_neigh, CONTRACT_COLS, preferred_element_type=F32)
        grad_mean = by_degree(grad_mean, inverse, b).astype(BF16)
        tile_copies[b].wait()
        parts = lax.dot_general(
            tile_row(tiles, b), grad_mean, CONTRACT_ROWS, preferred_element_type=F32
        )
        for p in range(npairs):
            entry = pairs_ref[b, p]
            entries[entry] = entries[entry] + parts[p * rows : (p + 1) * rows]

    own_ref[...] = entries[:nblocks]
    rims_ref[...] = entries[nblocks : nblocks + 2].astype(BF16)
    slots_ref[:, :rows, :] = entries[nblocks + 2 :].astype(BF16)
    slots_ref[:, rows:, :] = jnp.zeros(
        (slots_ref.shape[0], slots_ref.shape[1] - rows, width), BF16
    )


def combine_kernel(send_ref, own_ref, returned_ref, low_ref, high_ref, out_ref, total):
    total[...] = own_ref[...]
    last = total.shape[0] - 1
    total[0] = total[0] + low_ref[...].astype(F32)
    total[last] = total[last] + high_ref[...].astype(F32)
    for j in range(returned_ref.shape[0]):
        block = send_ref[0, j]
        total[block] = total[block] + returned_ref[j, : total.shape[1]].astype(F32)
    out_ref[...] = total[...].astype(BF16)


def call_forward(
    blocks, left, right, received, tiles, cot, pairs, degree, w_self, w_neigh, bias
):
    nblocks, npairs, rows, _ = tiles.shape
    width = blocks.shape[2]
    entries = nblocks + 2 + received.shape[0]
    shape = jax.ShapeDtypeStruct
    return pl.pallas_call(
        forward_kernel,
        out_shape=(
            shape(blocks.shape, BF16),
            shape((nblocks * rows, width), BF16),
            shape((2 * width, width), BF16),
            shape((1, width), F32),
        ),
        in_specs=[SMEM] + [VMEM] * 4 + [ANY] * 4 + [HBM] * 2,
        out_specs=(ANY, ANY, VMEM, VMEM),
        scratch_shapes=[
            pltpu.VMEM((entries, rows, width), BF16),
            pltpu.VMEM(tiles.shape, BF16),
            pltpu.VMEM(blocks.shape, BF16),
            pltpu.VMEM(blocks.shape, BF16),
            pltpu.VMEM((2, npairs * rows, width), BF16),
            pltpu.VMEM(blocks.shape, BF16),
            pltpu.VMEM((nblocks * rows, width), BF16),
            pltpu.VMEM((nblocks, rows, rows), F32),
            pltpu.SemaphoreType.DMA((7,)),
            pltpu.SemaphoreType.DMA((nblocks,)),
        ],
        compiler_params=params(58),
        cost_estimate=pl.CostEstimate(
            flops=2 * 10**9, bytes_accessed=6 * 10**6, transcendentals=nblocks * rows * width
        ),
    )(pairs, degree, w_self, w_neigh, bias, blocks, left, right, received, tiles, cot)


def call_backward(grad, tiles, pairs, degree, w_self, w_neigh):
    nblocks, _, rows, _ = tiles.shape
    width = w_self.shape[0]
    dom = lax.axis_size("dom")
    extra = 2 * width // lax.axis_size("inner") + 8
    shape = jax.ShapeDtypeStruct
    return pl.pallas_call(
        backward_kernel,
        out_shape=(
            shape((nblocks, rows, width), F32),
            shape((2, rows, width), BF16),
            shape((dom, rows + extra, width), BF16),
        ),
        in_specs=[SMEM] + [VMEM] * 4 + [HBM],
        out_specs=(VMEM,) * 3,
        scratch_shapes=[
            pltpu.VMEM(tiles.shape, BF16),
            pltpu.VMEM((nblocks, rows, rows), F32),
            pltpu.VMEM((nblocks + 2 + dom, rows, width), F32),
            pltpu.SemaphoreType.DMA((nblocks,)),
        ],
        compiler_params=params(),
        cost_estimate=pl.CostEstimate(
            flops=2 * 10**9, bytes_accessed=8 * 10**6, transcendentals=0
        ),
    )(pairs, degree, w_self, w_neigh, grad, tiles)


def neighbours(low_source, high_source, axis):
    count = lax.axis_size(axis)
    forward = [(i, i + 1) for i in range(count - 1)]
    backward = [(target, source) for source, target in forward]
    return lax.ppermute(low_source, axis, forward), lax.ppermute(high_source, axis, backward)


def merge_grads(grads, gbias, slots):
    inner_size = lax.axis_size("inner")
    hidden = grads.shape[1]
    chunks = grads.reshape(inner_size, grads.shape[0] // inner_size, hidden)
    pieces = lax.all_to_all(chunks, "inner", split_axis=0, concat_axis=0, tiled=True)
    return pl.pallas_call(
        merge_kernel,
        out_shape=jax.ShapeDtypeStruct(slots.shape, BF16),
        in_specs=[VMEM, VMEM, ANY],
        out_specs=ANY,
        scratch_shapes=[
            pltpu.VMEM((chunks.shape[1] + 8, hidden), BF16),
            pltpu.SemaphoreType.DMA((slots.shape[0],)),
        ],
        input_output_aliases={2: 0},
        compiler_params=params(),
    )(pieces, gbias, slots)


def spread_grads(extra, scale):
    inner_size = lax.axis_size("inner")
    hidden = extra.shape[2]
    rows = extra.shape[1] - 8
    summed = jnp.sum(extra.astype(F32), axis=0) * scale
    lanes = [summed[:rows, k : k + LANES] for k in range(0, hidden, LANES)]
    bias = (summed[rows] + summed[rows + 1]).reshape(-1, LANES)
    bias_rows = bias.shape[0]
    spare = jnp.zeros((8 - bias_rows, LANES), F32)
    piece = jnp.concatenate(lanes + [bias, spare], axis=0).astype(BF16)
    spread = jnp.broadcast_to(piece[None], (inner_size,) + piece.shape)
    spread = lax.all_to_all(spread, "inner", split_axis=0, concat_axis=0, tiled=True)
    return pl.pallas_call(
        functools.partial(unpack_kernel, rows, bias_rows),
        out_shape=(
            jax.ShapeDtypeStruct((hidden, hidden), F32),
            jax.ShapeDtypeStruct((hidden, hidden), F32),
            jax.ShapeDtypeStruct((bias_rows, LANES), F32),
        ),
        in_specs=[VMEM],
        out_specs=(VMEM,) * 3,
        compiler_params=params(),
    )(spread)


def unpack_kernel(rows, bias_rows, spread_ref, self_ref, neigh_ref, bias_ref):
    spread = spread_ref[...].astype(F32)
    half = spread.shape[0] // 2
    for k in range(bias_rows):
        part = spread[:, k * rows : (k + 1) * rows]
        for ref, first in ((self_ref, 0), (neigh_ref, half)):
            ref[:, k * LANES : (k + 1) * LANES] = part[first : first + half].reshape(-1, LANES)
    tail = jnp.sum(spread[:, bias_rows * rows :], axis=0)
    bias_ref[...] = tail[:bias_rows]


def per_device(
    features, tiles, pair_source, in_degree, send_blocks, w_self, w_neigh, bias, cotangent
):
    rows_dev, width = features.shape
    nblocks, _, rows, _ = tiles.shape
    dom_size = lax.axis_size("dom")
    blocks = features.reshape(nblocks, rows, width)
    outgoing = pl.pallas_call(
        pick_kernel,
        out_shape=jax.ShapeDtypeStruct((dom_size, rows, width), BF16),
        in_specs=[SMEM, HBM],
        out_specs=VMEM,
        scratch_shapes=[pltpu.SemaphoreType.DMA((dom_size,))],
        compiler_params=params(58),
    )(send_blocks, blocks)
    received = lax.all_to_all(outgoing, "dom", split_axis=0, concat_axis=0, tiled=True)
    left, right = neighbours(blocks[nblocks - 1], blocks[0], "inner")
    degree = in_degree.reshape(nblocks, rows)
    layer_out, grad_pre, grads, gbias = call_forward(
        blocks,
        left,
        right,
        received,
        tiles,
        cotangent.reshape(nblocks, rows, width),
        pair_source,
        degree,
        w_self,
        w_neigh,
        bias[None, :],
    )
    own, rims, slots = call_backward(grad_pre, tiles, pair_source, degree, w_self, w_neigh)
    merged = merge_grads(grads, gbias, slots)
    returned = lax.all_to_all(merged, "dom", split_axis=0, concat_axis=0, tiled=True)
    low, high = neighbours(rims[1], rims[0], "inner")
    extra, low, high = lax.optimization_barrier((returned[:, rows:], low, high))
    grad_features = pl.pallas_call(
        combine_kernel,
        out_shape=jax.ShapeDtypeStruct(blocks.shape, BF16),
        in_specs=[SMEM] + [VMEM] * 4,
        out_specs=VMEM,
        scratch_shapes=[pltpu.VMEM(blocks.shape, F32)],
        compiler_params=params(),
        cost_estimate=pl.CostEstimate(
            flops=10**6, bytes_accessed=3 * 10**6, transcendentals=0
        ),
    )(send_blocks, own, returned, low, high)
    scale = 1.0 / math.sqrt(rows_dev * dom_size * lax.axis_size("inner"))
    sum_self, sum_neigh, sum_bias = spread_grads(extra, scale)
    return (
        layer_out.reshape(rows_dev, width),
        grad_features.reshape(rows_dev, width),
        sum_self,
        sum_neigh,
        sum_bias.reshape(-1),
    )


def solution(mesh):
    return jax.shard_map(
        per_device,
        mesh=mesh,
        in_specs=(
            P(("dom", "inner"), None),
            P(("dom", "inner"), None, None, None),
            P(("dom", "inner"), None),
            P(("dom", "inner")),
            P(("dom", "inner"), None),
            P(),
            P(),
            P(),
            P(("dom", "inner"), None),
        ),
        out_specs=(P(("dom", "inner"), None), P(("dom", "inner"), None), P(), P(), P()),
        check_vma=False,
    )
```

```python
import functools
import math

import jax
import jax.numpy as jnp
from jax import lax
from jax.experimental import pallas as pl
from jax.experimental.pallas import tpu as pltpu
from jax.sharding import PartitionSpec as P

LANES = 128
VMEM = pl.BlockSpec(memory_space=pltpu.VMEM)
SMEM = pl.BlockSpec(memory_space=pltpu.SMEM)
ANY = pl.BlockSpec(memory_space=pl.ANY)
HBM = pl.BlockSpec(memory_space=pltpu.HBM)
F32 = jnp.float32
BF16 = jnp.bfloat16
CONTRACT_ROWS = (((0,), (0,)), ((), ()))
CONTRACT_COLS = (((1,), (1,)), ((), ()))


def params(mebibytes=32):
    return pltpu.CompilerParams(vmem_limit_bytes=mebibytes * 1024 * 1024)


def pick_kernel(send_ref, blocks_ref, out_ref, sems):
    copies = [
        pltpu.make_async_copy(blocks_ref.at[send_ref[0, j]], out_ref.at[j], sems.at[j])
        for j in range(out_ref.shape[0])
    ]
    for copy in copies:
        copy.start()
    for copy in copies:
        copy.wait()


def split_bias(bias):
    high = bias.astype(BF16).astype(F32)
    return [high, bias - high]


def piece_kernel(pieces_ref, gbias_ref, out_ref):
    summed = jnp.sum(pieces_ref[...].astype(F32), axis=0)
    hidden = summed.shape[1]
    lanes = [summed[:, k : k + LANES] for k in range(0, hidden, LANES)]
    bias = [gbias_ref[:, k : k + LANES] for k in range(0, hidden, LANES)]
    tail = split_bias(jnp.concatenate(bias, axis=0))
    tail.append(jnp.zeros((out_ref.shape[1] // 2 - 2 * len(bias), LANES), F32))
    piece = jnp.concatenate(lanes + tail, axis=0).astype(BF16)
    out_ref[...] = jnp.broadcast_to(piece[None], out_ref.shape)


def start_kernel(scale, spread_ref, out_ref):
    rows = out_ref.shape[1]
    bias_rows = 2
    summed = jnp.sum(spread_ref[...].astype(F32), axis=0) * scale
    out_ref[0] = summed[:rows].astype(BF16)
    tail = summed[rows:]
    bias = tail[:bias_rows] + tail[bias_rows : 2 * bias_rows]
    spare = jnp.zeros((rows - 2 * bias_rows, LANES), F32)
    out_ref[1] = jnp.concatenate(split_bias(bias) + [spare], axis=0).astype(BF16)


def double_kernel(shift, place_ref, mine_ref, theirs_ref, out_ref):
    count = mine_ref.shape[0] - 1
    bit = lax.bitwise_and(lax.shift_right_logical(place_ref[0], shift), 1)
    out_ref[pl.ds(bit * count, count)] = mine_ref[:count]
    out_ref[pl.ds((1 - bit) * count, count)] = theirs_ref[:count]
    tail = mine_ref[count].astype(F32) + theirs_ref[count].astype(F32)
    bias_rows = 2
    bias = tail[:bias_rows] + tail[bias_rows : 2 * bias_rows]
    spare = jnp.zeros((tail.shape[0] - 2 * bias_rows, LANES), F32)
    out_ref[2 * count] = jnp.concatenate(split_bias(bias) + [spare], axis=0).astype(BF16)


def tile_row(tiles, b):
    return jnp.concatenate([tiles[b, p] for p in range(tiles.shape[1])], axis=1)


def by_degree(values, inverse, b):
    rows = inverse.shape[1]
    return jnp.concatenate(
        [values[:, k : k + rows] * inverse[b] for k in range(0, values.shape[1], rows)], axis=1
    )


def invert_degree(degree_ref, inverse):
    for b in range(inverse.shape[0]):
        row = 1.0 / degree_ref[b : b + 1, :].astype(F32)
        inverse[b] = jnp.broadcast_to(row, inverse.shape[1:]).T


def forward_kernel(
    pairs_ref,
    degree_ref,
    w_self_ref,
    w_neigh_ref,
    bias_ref,
    blocks_hbm,
    left_ref,
    right_ref,
    received_hbm,
    tiles_hbm,
    cot_hbm,
    out_hbm,
    grad_hbm,
    grads_ref,
    gbias_ref,
    table,
    tiles,
    cot,
    out,
    sources,
    mean,
    grad_pre,
    inverse,
    sems,
    tile_sems,
):
    nblocks, npairs, rows, _ = tiles.shape
    width = table.shape[2]
    copies = [
        pltpu.make_async_copy(blocks_hbm, table.at[pl.ds(0, nblocks)], sems.at[0]),
        pltpu.make_async_copy(
            received_hbm, table.at[pl.ds(nblocks + 2, received_hbm.shape[0])], sems.at[1]
        ),
    ]
    tile_copies = [
        pltpu.make_async_copy(tiles_hbm.at[b], tiles.at[b], tile_sems.at[b])
        for b in range(nblocks)
    ]
    cot_copy = pltpu.make_async_copy(cot_hbm, cot, sems.at[2])
    out_copy = pltpu.make_async_copy(out, out_hbm, sems.at[3])
    grad_copy = pltpu.make_async_copy(grad_pre, grad_hbm, sems.at[4])
    for copy in copies:
        copy.start()
    for copy in tile_copies:
        copy.start()
    cot_copy.start()
    table[nblocks] = left_ref[...]
    table[nblocks + 1] = right_ref[...]
    invert_degree(degree_ref, inverse)
    for copy in copies:
        copy.wait()

    for b in range(nblocks):
        for p in range(npairs):
            sources[b % 2, pl.ds(p * rows, rows), :] = table[pairs_ref[b, p]]
        tile_copies[b].wait()
        summed = jnp.dot(tile_row(tiles, b), sources[b % 2], preferred_element_type=F32)
        mean[b] = by_degree(summed, inverse, b).astype(BF16)

    cot_copy.wait()
    w_self = w_self_ref[...]
    w_neigh = w_neigh_ref[...]
    gbias = jnp.zeros((1, width), F32)
    step = 2
    for b in range(0, nblocks, step):
        features = table[b : b + step].reshape(step * rows, width)
        means = mean[b : b + step].reshape(step * rows, width)
        preact = (
            jnp.dot(features, w_self, preferred_element_type=F32)
            + jnp.dot(means, w_neigh, preferred_element_type=F32)
            + bias_ref[...]
        )
        sigma = jax.nn.sigmoid(preact)
        out[b : b + step] = (preact * sigma).astype(BF16).reshape(step, rows, width)
        cots = cot[b : b + step].reshape(step * rows, width).astype(F32)
        grad = (cots * sigma * (1.0 + preact * (1.0 - sigma))).astype(BF16)
        grad_pre[pl.ds(b * rows, step * rows), :] = grad
        gbias = gbias + jnp.sum(grad.astype(F32), axis=0, keepdims=True)
    grad_copy.start()
    out_copy.start()
    gbias_ref[...] = gbias

    grads = grad_pre[...]
    features = table[:nblocks].reshape(nblocks * rows, width)
    means = mean[...].reshape(nblocks * rows, width)
    grads_ref[:width, :] = lax.dot_general(
        features, grads, CONTRACT_ROWS, preferred_element_type=F32
    ).astype(BF16)
    grads_ref[width:, :] = lax.dot_general(
        means, grads, CONTRACT_ROWS, preferred_element_type=F32
    ).astype(BF16)
    grad_copy.wait()
    out_copy.wait()


def backward_kernel(
    pairs_ref,
    degree_ref,
    w_self_ref,
    w_neigh_ref,
    grad_ref,
    tiles_hbm,
    own_ref,
    rims_ref,
    slots_ref,
    tiles,
    inverse,
    entries,
    tile_sems,
):
    nblocks, npairs, rows, _ = tiles.shape
    width = w_self_ref.shape[0]
    tile_copies = [
        pltpu.make_async_copy(tiles_hbm.at[b], tiles.at[b], tile_sems.at[b])
        for b in range(nblocks)
    ]
    for copy in tile_copies:
        copy.start()
    invert_degree(degree_ref, inverse)
    entries[nblocks:] = jnp.zeros((entries.shape[0] - nblocks, rows, width), F32)
    w_self = w_self_ref[...]
    w_neigh = w_neigh_ref[...]
    own = lax.dot_general(grad_ref[...], w_self, CONTRACT_COLS, preferred_element_type=F32)
    entries[:nblocks] = own.reshape(nblocks, rows, width)
    for b in range(nblocks):
        grad = grad_ref[pl.ds(b * rows, rows), :]
        grad_mean = lax.dot_general(grad, w_neigh, CONTRACT_COLS, preferred_element_type=F32)
        grad_mean = by_degree(grad_mean, inverse, b).astype(BF16)
        tile_copies[b].wait()
        parts = lax.dot_general(
            tile_row(tiles, b), grad_mean, CONTRACT_ROWS, preferred_element_type=F32
        )
        for p in range(npairs):
            entry = pairs_ref[b, p]
            entries[entry] = entries[entry] + parts[p * rows : (p + 1) * rows]

    own_ref[...] = entries[:nblocks]
    rims_ref[...] = entries[nblocks : nblocks + 2].astype(BF16)
    slots_ref[...] = entries[nblocks + 2 :].astype(BF16)


def combine_kernel(send_ref, own_ref, returned_ref, low_ref, high_ref, out_ref, total):
    total[...] = own_ref[...]
    last = total.shape[0] - 1
    total[0] = total[0] + low_ref[...].astype(F32)
    total[last] = total[last] + high_ref[...].astype(F32)
    for j in range(returned_ref.shape[0]):
        block = send_ref[0, j]
        total[block] = total[block] + returned_ref[j].astype(F32)
    out_ref[...] = total[...].astype(BF16)


def call_forward(
    blocks, left, right, received, tiles, cot, pairs, degree, w_self, w_neigh, bias
):
    nblocks, npairs, rows, _ = tiles.shape
    width = blocks.shape[2]
    entries = nblocks + 2 + received.shape[0]
    shape = jax.ShapeDtypeStruct
    return pl.pallas_call(
        forward_kernel,
        out_shape=(
            shape(blocks.shape, BF16),
            shape((nblocks * rows, width), BF16),
            shape((2 * width, width), BF16),
            shape((1, width), F32),
        ),
        in_specs=[SMEM] + [VMEM] * 4 + [HBM, VMEM, VMEM, ANY, HBM, HBM],
        out_specs=(ANY, ANY, VMEM, VMEM),
        scratch_shapes=[
            pltpu.VMEM((entries, rows, width), BF16),
            pltpu.VMEM(tiles.shape, BF16),
            pltpu.VMEM(blocks.shape, BF16),
            pltpu.VMEM(blocks.shape, BF16),
            pltpu.VMEM((2, npairs * rows, width), BF16),
            pltpu.VMEM(blocks.shape, BF16),
            pltpu.VMEM((nblocks * rows, width), BF16),
            pltpu.VMEM((nblocks, rows, rows), F32),
            pltpu.SemaphoreType.DMA((5,)),
            pltpu.SemaphoreType.DMA((nblocks,)),
        ],
        compiler_params=params(58),
        cost_estimate=pl.CostEstimate(
            flops=2 * 10**9, bytes_accessed=6 * 10**6, transcendentals=nblocks * rows * width
        ),
    )(pairs, degree, w_self, w_neigh, bias, blocks, left, right, received, tiles, cot)


def call_backward(grad, tiles, pairs, degree, w_self, w_neigh):
    nblocks, _, rows, _ = tiles.shape
    width = w_self.shape[0]
    dom = lax.axis_size("dom")
    shape = jax.ShapeDtypeStruct
    return pl.pallas_call(
        backward_kernel,
        out_shape=(
            shape((nblocks, rows, width), F32),
            shape((2, rows, width), BF16),
            shape((dom, rows, width), BF16),
        ),
        in_specs=[SMEM] + [VMEM] * 4 + [HBM],
        out_specs=(VMEM,) * 3,
        scratch_shapes=[
            pltpu.VMEM(tiles.shape, BF16),
            pltpu.VMEM((nblocks, rows, rows), F32),
            pltpu.VMEM((nblocks + 2 + dom, rows, width), F32),
            pltpu.SemaphoreType.DMA((nblocks,)),
        ],
        compiler_params=params(),
        cost_estimate=pl.CostEstimate(
            flops=2 * 10**9, bytes_accessed=8 * 10**6, transcendentals=0
        ),
    )(pairs, degree, w_self, w_neigh, grad, tiles)


def neighbours(low_source, high_source, axis):
    count = lax.axis_size(axis)
    forward = [(i, i + 1) for i in range(count - 1)]
    backward = [(target, source) for source, target in forward]
    return lax.ppermute(low_source, axis, forward), lax.ppermute(high_source, axis, backward)


def reduce_grads(grads, gbias, scale):
    dom_size = lax.axis_size("dom")
    inner_size = lax.axis_size("inner")
    hidden = grads.shape[1]
    chunks = grads.reshape(inner_size, grads.shape[0] // inner_size, hidden)
    pieces = lax.all_to_all(chunks, "inner", split_axis=0, concat_axis=0, tiled=True)
    rows = chunks.shape[1] * chunks.shape[2] // LANES
    spread = pl.pallas_call(
        piece_kernel,
        out_shape=jax.ShapeDtypeStruct((dom_size, 2 * rows, LANES), BF16),
        in_specs=[VMEM, VMEM],
        out_specs=VMEM,
        compiler_params=params(),
    )(pieces, gbias)
    spread = lax.all_to_all(spread, "dom", split_axis=0, concat_axis=0, tiled=True)
    return pl.pallas_call(
        functools.partial(start_kernel, scale),
        out_shape=jax.ShapeDtypeStruct((2, rows, LANES), BF16),
        in_specs=[VMEM],
        out_specs=VMEM,
        compiler_params=params(),
    )(spread)


def gather_grads(state, hidden):
    inner_size = lax.axis_size("inner")
    shifts = list(reversed(range(inner_size.bit_length() - 1)))
    index = lax.axis_index("inner").astype(jnp.int32).reshape(1)
    for shift in shifts:
        pairs = [(i, i ^ (1 << shift)) for i in range(inner_size)]
        theirs = lax.ppermute(state, "inner", pairs)
        count = 2 * (state.shape[0] - 1) + 1
        state = pl.pallas_call(
            functools.partial(double_kernel, shift),
            out_shape=jax.ShapeDtypeStruct((count,) + state.shape[1:], BF16),
            in_specs=[SMEM, VMEM, VMEM],
            out_specs=VMEM,
            compiler_params=params(),
        )(index, state, theirs)
    place = []
    for chunk in range(inner_size):
        place.append(sum(((chunk >> shift) % 2) << k for k, shift in enumerate(shifts)))
    return pl.pallas_call(
        functools.partial(unpack_kernel, place),
        out_shape=(
            jax.ShapeDtypeStruct((hidden, hidden), F32),
            jax.ShapeDtypeStruct((hidden, hidden), F32),
            jax.ShapeDtypeStruct((2, LANES), F32),
        ),
        in_specs=[VMEM],
        out_specs=(VMEM,) * 3,
        compiler_params=params(),
    )(state)


def unpack_kernel(place, state_ref, self_ref, neigh_ref, bias_ref):
    hidden = self_ref.shape[1]
    groups = hidden // LANES
    rows = state_ref.shape[1] // groups
    half = len(place) // 2
    for chunk, where in enumerate(place):
        ref = self_ref if chunk < half else neigh_ref
        first = (chunk % half) * rows
        values = state_ref[where].astype(F32)
        for k in range(groups):
            ref[first : first + rows, k * LANES : (k + 1) * LANES] = values[
                k * rows : (k + 1) * rows
            ]
    tail = state_ref[len(place)].astype(F32)
    bias_ref[...] = tail[:groups] + tail[groups : 2 * groups]


def per_device(
    features, tiles, pair_source, in_degree, send_blocks, w_self, w_neigh, bias, cotangent
):
    rows_dev, width = features.shape
    nblocks, _, rows, _ = tiles.shape
    dom_size = lax.axis_size("dom")
    blocks = features.reshape(nblocks, rows, width)
    outgoing = pl.pallas_call(
        pick_kernel,
        out_shape=jax.ShapeDtypeStruct((dom_size, rows, width), BF16),
        in_specs=[SMEM, HBM],
        out_specs=VMEM,
        scratch_shapes=[pltpu.SemaphoreType.DMA((dom_size,))],
        compiler_params=params(58),
    )(send_blocks, blocks)
    received = lax.all_to_all(outgoing, "dom", split_axis=0, concat_axis=0, tiled=True)
    left, right = neighbours(blocks[nblocks - 1], blocks[0], "inner")
    degree = in_degree.reshape(nblocks, rows)
    layer_out, grad_pre, grads, gbias = call_forward(
        blocks,
        left,
        right,
        received,
        tiles,
        cotangent.reshape(nblocks, rows, width),
        pair_source,
        degree,
        w_self,
        w_neigh,
        bias[None, :],
    )
    own, rims, slots = call_backward(grad_pre, tiles, pair_source, degree, w_self, w_neigh)
    low, high = neighbours(rims[1], rims[0], "inner")
    scale = 1.0 / math.sqrt(rows_dev * dom_size * lax.axis_size("inner"))
    state = reduce_grads(grads, gbias, scale)
    state, slots, low, high = lax.optimization_barrier((state, slots, low, high))
    returned = lax.all_to_all(slots, "dom", split_axis=0, concat_axis=0, tiled=True)
    sum_self, sum_neigh, sum_bias = gather_grads(state, width)
    grad_features = pl.pallas_call(
        combine_kernel,
        out_shape=jax.ShapeDtypeStruct(blocks.shape, BF16),
        in_specs=[SMEM] + [VMEM] * 4,
        out_specs=VMEM,
        scratch_shapes=[pltpu.VMEM(blocks.shape, F32)],
        compiler_params=params(),
        cost_estimate=pl.CostEstimate(
            flops=10**6, bytes_accessed=3 * 10**6, transcendentals=0
        ),
    )(send_blocks, own, returned, low, high)
    return (
        layer_out.reshape(rows_dev, width),
        grad_features.reshape(rows_dev, width),
        sum_self,
        sum_neigh,
        sum_bias.reshape(-1),
    )


def solution(mesh):
    return jax.shard_map(
        per_device,
        mesh=mesh,
        in_specs=(
            P(("dom", "inner"), None),
            P(("dom", "inner"), None, None, None),
            P(("dom", "inner"), None),
            P(("dom", "inner")),
            P(("dom", "inner"), None),
            P(),
            P(),
            P(),
            P(("dom", "inner"), None),
        ),
        out_specs=(P(("dom", "inner"), None), P(("dom", "inner"), None), P(), P(), P()),
        check_vma=False,
    )
```

```python
import functools
import math

import jax
import jax.numpy as jnp
from jax import lax
from jax.experimental import pallas as pl
from jax.experimental.pallas import tpu as pltpu
from jax.sharding import PartitionSpec as P

LANES = 128
VMEM = pl.BlockSpec(memory_space=pltpu.VMEM)
SMEM = pl.BlockSpec(memory_space=pltpu.SMEM)
ANY = pl.BlockSpec(memory_space=pl.ANY)
HBM = pl.BlockSpec(memory_space=pltpu.HBM)
F32 = jnp.float32
BF16 = jnp.bfloat16
CONTRACT_ROWS = (((0,), (0,)), ((), ()))
CONTRACT_COLS = (((1,), (1,)), ((), ()))


def params(mebibytes=32):
    return pltpu.CompilerParams(vmem_limit_bytes=mebibytes * 1024 * 1024)


def pick_kernel(send_ref, blocks_ref, out_ref, sems):
    copies = [
        pltpu.make_async_copy(blocks_ref.at[send_ref[0, j]], out_ref.at[j], sems.at[j])
        for j in range(out_ref.shape[0])
    ]
    for copy in copies:
        copy.start()
    for copy in copies:
        copy.wait()


def split_bias(bias):
    high = bias.astype(BF16).astype(F32)
    return [high, bias - high]


def piece_kernel(pieces_ref, gbias_ref, out_ref):
    summed = jnp.sum(pieces_ref[...].astype(F32), axis=0)
    hidden = summed.shape[1]
    lanes = [summed[:, k : k + LANES] for k in range(0, hidden, LANES)]
    bias = [gbias_ref[:, k : k + LANES] for k in range(0, hidden, LANES)]
    tail = split_bias(jnp.concatenate(bias, axis=0))
    tail.append(jnp.zeros((out_ref.shape[1] // 2 - 2 * len(bias), LANES), F32))
    piece = jnp.concatenate(lanes + tail, axis=0).astype(BF16)
    out_ref[...] = jnp.broadcast_to(piece[None], out_ref.shape)


def start_kernel(scale, spread_ref, out_ref):
    rows = out_ref.shape[1]
    bias_rows = 2
    summed = jnp.sum(spread_ref[...].astype(F32), axis=0) * scale
    out_ref[0] = summed[:rows].astype(BF16)
    tail = summed[rows:]
    bias = tail[:bias_rows] + tail[bias_rows : 2 * bias_rows]
    spare = jnp.zeros((rows - 2 * bias_rows, LANES), F32)
    out_ref[1] = jnp.concatenate(split_bias(bias) + [spare], axis=0).astype(BF16)


def grow_kernel(low, place_ref, mine_ref, *refs):
    theirs_refs, out_ref = refs[:-1], refs[-1]
    count = mine_ref.shape[0] - 1
    value = lax.bitwise_and(lax.shift_right_logical(place_ref[0], low), len(theirs_refs))
    out_ref[pl.ds(value * count, count)] = mine_ref[:count]
    tail = mine_ref[count].astype(F32)
    for mask, theirs_ref in enumerate(theirs_refs, 1):
        other = lax.bitwise_xor(value, mask)
        out_ref[pl.ds(other * count, count)] = theirs_ref[:count]
        tail = tail + theirs_ref[count].astype(F32)
    bias_rows = 2
    bias = tail[:bias_rows] + tail[bias_rows : 2 * bias_rows]
    spare = jnp.zeros((tail.shape[0] - 2 * bias_rows, LANES), F32)
    last = out_ref.shape[0] - 1
    out_ref[last] = jnp.concatenate(split_bias(bias) + [spare], axis=0).astype(BF16)


def tile_row(tiles, b):
    return jnp.concatenate([tiles[b, p] for p in range(tiles.shape[1])], axis=1)


def by_degree(values, inverse, b):
    rows = inverse.shape[1]
    return jnp.concatenate(
        [values[:, k : k + rows] * inverse[b] for k in range(0, values.shape[1], rows)], axis=1
    )


def invert_degree(degree_ref, inverse):
    for b in range(inverse.shape[0]):
        row = 1.0 / degree_ref[b : b + 1, :].astype(F32)
        inverse[b] = jnp.broadcast_to(row, inverse.shape[1:]).T


def forward_kernel(
    pairs_ref,
    degree_ref,
    w_self_ref,
    w_neigh_ref,
    bias_ref,
    blocks_hbm,
    left_ref,
    right_ref,
    received_hbm,
    tiles_hbm,
    cot_hbm,
    out_hbm,
    grad_hbm,
    grads_ref,
    gbias_ref,
    table,
    tiles,
    cot,
    out,
    sources,
    mean,
    grad_pre,
    inverse,
    sems,
    tile_sems,
):
    nblocks, npairs, rows, _ = tiles.shape
    width = table.shape[2]
    copies = [
        pltpu.make_async_copy(blocks_hbm, table.at[pl.ds(0, nblocks)], sems.at[0]),
        pltpu.make_async_copy(
            received_hbm, table.at[pl.ds(nblocks + 2, received_hbm.shape[0])], sems.at[1]
        ),
    ]
    tile_copies = [
        pltpu.make_async_copy(tiles_hbm.at[b], tiles.at[b], tile_sems.at[b])
        for b in range(nblocks)
    ]
    cot_copy = pltpu.make_async_copy(cot_hbm, cot, sems.at[2])
    out_copy = pltpu.make_async_copy(out, out_hbm, sems.at[3])
    grad_copy = pltpu.make_async_copy(grad_pre, grad_hbm, sems.at[4])
    for copy in copies:
        copy.start()
    for copy in tile_copies:
        copy.start()
    cot_copy.start()
    table[nblocks] = left_ref[...]
    table[nblocks + 1] = right_ref[...]
    invert_degree(degree_ref, inverse)
    for copy in copies:
        copy.wait()

    for b in range(nblocks):
        for p in range(npairs):
            sources[b % 2, pl.ds(p * rows, rows), :] = table[pairs_ref[b, p]]
        tile_copies[b].wait()
        summed = jnp.dot(tile_row(tiles, b), sources[b % 2], preferred_element_type=F32)
        mean[b] = by_degree(summed, inverse, b).astype(BF16)

    cot_copy.wait()
    w_self = w_self_ref[...]
    w_neigh = w_neigh_ref[...]
    gbias = jnp.zeros((1, width), F32)
    step = 2
    for b in range(0, nblocks, step):
        features = table[b : b + step].reshape(step * rows, width)
        means = mean[b : b + step].reshape(step * rows, width)
        preact = (
            jnp.dot(features, w_self, preferred_element_type=F32)
            + jnp.dot(means, w_neigh, preferred_element_type=F32)
            + bias_ref[...]
        )
        sigma = jax.nn.sigmoid(preact)
        out[b : b + step] = (preact * sigma).astype(BF16).reshape(step, rows, width)
        cots = cot[b : b + step].reshape(step * rows, width).astype(F32)
        grad = (cots * sigma * (1.0 + preact * (1.0 - sigma))).astype(BF16)
        grad_pre[pl.ds(b * rows, step * rows), :] = grad
        gbias = gbias + jnp.sum(grad.astype(F32), axis=0, keepdims=True)
    grad_copy.start()
    out_copy.start()
    gbias_ref[...] = gbias

    grads = grad_pre[...]
    features = table[:nblocks].reshape(nblocks * rows, width)
    means = mean[...].reshape(nblocks * rows, width)
    grads_ref[:width, :] = lax.dot_general(
        features, grads, CONTRACT_ROWS, preferred_element_type=F32
    ).astype(BF16)
    grads_ref[width:, :] = lax.dot_general(
        means, grads, CONTRACT_ROWS, preferred_element_type=F32
    ).astype(BF16)
    grad_copy.wait()
    out_copy.wait()


def backward_kernel(
    pairs_ref,
    degree_ref,
    w_self_ref,
    w_neigh_ref,
    grad_ref,
    tiles_hbm,
    own_ref,
    rims_ref,
    slots_ref,
    tiles,
    inverse,
    entries,
    tile_sems,
):
    nblocks, npairs, rows, _ = tiles.shape
    width = w_self_ref.shape[0]
    tile_copies = [
        pltpu.make_async_copy(tiles_hbm.at[b], tiles.at[b], tile_sems.at[b])
        for b in range(nblocks)
    ]
    for copy in tile_copies:
        copy.start()
    invert_degree(degree_ref, inverse)
    entries[nblocks:] = jnp.zeros((entries.shape[0] - nblocks, rows, width), F32)
    w_self = w_self_ref[...]
    w_neigh = w_neigh_ref[...]
    own = lax.dot_general(grad_ref[...], w_self, CONTRACT_COLS, preferred_element_type=F32)
    entries[:nblocks] = own.reshape(nblocks, rows, width)
    for b in range(nblocks):
        grad = grad_ref[pl.ds(b * rows, rows), :]
        grad_mean = lax.dot_general(grad, w_neigh, CONTRACT_COLS, preferred_element_type=F32)
        grad_mean = by_degree(grad_mean, inverse, b).astype(BF16)
        tile_copies[b].wait()
        parts = lax.dot_general(
            tile_row(tiles, b), grad_mean, CONTRACT_ROWS, preferred_element_type=F32
        )
        for p in range(npairs):
            entry = pairs_ref[b, p]
            entries[entry] = entries[entry] + parts[p * rows : (p + 1) * rows]

    own_ref[...] = entries[:nblocks]
    rims_ref[...] = entries[nblocks : nblocks + 2].astype(BF16)
    slots_ref[...] = entries[nblocks + 2 :].astype(BF16)


def combine_kernel(send_ref, own_ref, returned_ref, low_ref, high_ref, out_ref, total):
    total[...] = own_ref[...]
    last = total.shape[0] - 1
    total[0] = total[0] + low_ref[...].astype(F32)
    total[last] = total[last] + high_ref[...].astype(F32)
    for j in range(returned_ref.shape[0]):
        block = send_ref[0, j]
        total[block] = total[block] + returned_ref[j].astype(F32)
    out_ref[...] = total[...].astype(BF16)


def call_forward(
    blocks, left, right, received, tiles, cot, pairs, degree, w_self, w_neigh, bias
):
    nblocks, npairs, rows, _ = tiles.shape
    width = blocks.shape[2]
    entries = nblocks + 2 + received.shape[0]
    shape = jax.ShapeDtypeStruct
    return pl.pallas_call(
        forward_kernel,
        out_shape=(
            shape(blocks.shape, BF16),
            shape((nblocks * rows, width), BF16),
            shape((2 * width, width), BF16),
            shape((1, width), F32),
        ),
        in_specs=[SMEM] + [VMEM] * 4 + [HBM, VMEM, VMEM, ANY, HBM, HBM],
        out_specs=(ANY, ANY, VMEM, VMEM),
        scratch_shapes=[
            pltpu.VMEM((entries, rows, width), BF16),
            pltpu.VMEM(tiles.shape, BF16),
            pltpu.VMEM(blocks.shape, BF16),
            pltpu.VMEM(blocks.shape, BF16),
            pltpu.VMEM((2, npairs * rows, width), BF16),
            pltpu.VMEM(blocks.shape, BF16),
            pltpu.VMEM((nblocks * rows, width), BF16),
            pltpu.VMEM((nblocks, rows, rows), F32),
            pltpu.SemaphoreType.DMA((5,)),
            pltpu.SemaphoreType.DMA((nblocks,)),
        ],
        compiler_params=params(58),
        cost_estimate=pl.CostEstimate(
            flops=2 * 10**9, bytes_accessed=6 * 10**6, transcendentals=nblocks * rows * width
        ),
    )(pairs, degree, w_self, w_neigh, bias, blocks, left, right, received, tiles, cot)


def call_backward(grad, tiles, pairs, degree, w_self, w_neigh):
    nblocks, _, rows, _ = tiles.shape
    width = w_self.shape[0]
    dom = lax.axis_size("dom")
    shape = jax.ShapeDtypeStruct
    return pl.pallas_call(
        backward_kernel,
        out_shape=(
            shape((nblocks, rows, width), F32),
            shape((2, rows, width), BF16),
            shape((dom, rows, width), BF16),
        ),
        in_specs=[SMEM] + [VMEM] * 4 + [HBM],
        out_specs=(VMEM,) * 3,
        scratch_shapes=[
            pltpu.VMEM(tiles.shape, BF16),
            pltpu.VMEM((nblocks, rows, rows), F32),
            pltpu.VMEM((nblocks + 2 + dom, rows, width), F32),
            pltpu.SemaphoreType.DMA((nblocks,)),
        ],
        compiler_params=params(58),
        cost_estimate=pl.CostEstimate(
            flops=2 * 10**9, bytes_accessed=8 * 10**6, transcendentals=0
        ),
    )(pairs, degree, w_self, w_neigh, grad, tiles)


def neighbours(low_source, high_source, axis):
    count = lax.axis_size(axis)
    forward = [(i, i + 1) for i in range(count - 1)]
    backward = [(target, source) for source, target in forward]
    return lax.ppermute(low_source, axis, forward), lax.ppermute(high_source, axis, backward)


def reduce_grads(grads, gbias, scale):
    dom_size = lax.axis_size("dom")
    inner_size = lax.axis_size("inner")
    hidden = grads.shape[1]
    chunks = grads.reshape(inner_size, grads.shape[0] // inner_size, hidden)
    pieces = lax.all_to_all(chunks, "inner", split_axis=0, concat_axis=0, tiled=True)
    rows = chunks.shape[1] * chunks.shape[2] // LANES
    spread = pl.pallas_call(
        piece_kernel,
        out_shape=jax.ShapeDtypeStruct((dom_size, 2 * rows, LANES), BF16),
        in_specs=[VMEM, VMEM],
        out_specs=VMEM,
        compiler_params=params(),
    )(pieces, gbias)
    spread = lax.all_to_all(spread, "dom", split_axis=0, concat_axis=0, tiled=True)
    return pl.pallas_call(
        functools.partial(start_kernel, scale),
        out_shape=jax.ShapeDtypeStruct((2, rows, LANES), BF16),
        in_specs=[VMEM],
        out_specs=VMEM,
        compiler_params=params(),
    )(spread)


def gather_grads(state, hidden):
    inner_size = lax.axis_size("inner")
    bits = inner_size.bit_length() - 1
    groups = ((3, 1), (4, 2), (1, 2), (0, 1)) if bits == 6 else ((0, bits),)
    index = lax.axis_index("inner").astype(jnp.int32).reshape(1)
    place = [0] * inner_size
    for low, size in groups:
        count = state.shape[0] - 1
        theirs = []
        for mask in range(1, 1 << size):
            pairs = [(i, i ^ (mask << low)) for i in range(inner_size)]
            theirs.append(lax.ppermute(state, "inner", pairs))
        place = [
            where + ((chunk >> low) % (1 << size)) * count for chunk, where in enumerate(place)
        ]
        state = pl.pallas_call(
            functools.partial(grow_kernel, low),
            out_shape=jax.ShapeDtypeStruct(((count << size) + 1,) + state.shape[1:], BF16),
            in_specs=[SMEM] + [VMEM] * (1 + len(theirs)),
            out_specs=VMEM,
            compiler_params=params(),
        )(index, state, *theirs)
    return pl.pallas_call(
        functools.partial(unpack_kernel, place),
        out_shape=(
            jax.ShapeDtypeStruct((hidden, hidden), F32),
            jax.ShapeDtypeStruct((hidden, hidden), F32),
            jax.ShapeDtypeStruct((2, LANES), F32),
        ),
        in_specs=[VMEM],
        out_specs=(VMEM,) * 3,
        compiler_params=params(),
    )(state)


def unpack_kernel(place, state_ref, self_ref, neigh_ref, bias_ref):
    hidden = self_ref.shape[1]
    groups = hidden // LANES
    rows = state_ref.shape[1] // groups
    half = len(place) // 2
    for chunk, where in enumerate(place):
        ref = self_ref if chunk < half else neigh_ref
        first = (chunk % half) * rows
        values = state_ref[where].astype(F32)
        for k in range(groups):
            ref[first : first + rows, k * LANES : (k + 1) * LANES] = values[
                k * rows : (k + 1) * rows
            ]
    tail = state_ref[len(place)].astype(F32)
    bias_ref[...] = tail[:groups] + tail[groups : 2 * groups]


def per_device(
    features, tiles, pair_source, in_degree, send_blocks, w_self, w_neigh, bias, cotangent
):
    rows_dev, width = features.shape
    nblocks, _, rows, _ = tiles.shape
    dom_size = lax.axis_size("dom")
    blocks = features.reshape(nblocks, rows, width)
    outgoing = pl.pallas_call(
        pick_kernel,
        out_shape=jax.ShapeDtypeStruct((dom_size, rows, width), BF16),
        in_specs=[SMEM, HBM],
        out_specs=VMEM,
        scratch_shapes=[pltpu.SemaphoreType.DMA((dom_size,))],
        compiler_params=params(58),
    )(send_blocks, blocks)
    received = lax.all_to_all(outgoing, "dom", split_axis=0, concat_axis=0, tiled=True)
    left, right = neighbours(blocks[nblocks - 1], blocks[0], "inner")
    degree = in_degree.reshape(nblocks, rows)
    layer_out, grad_pre, grads, gbias = call_forward(
        blocks,
        left,
        right,
        received,
        tiles,
        cotangent.reshape(nblocks, rows, width),
        pair_source,
        degree,
        w_self,
        w_neigh,
        bias[None, :],
    )
    own, rims, slots = call_backward(grad_pre, tiles, pair_source, degree, w_self, w_neigh)
    low, high = neighbours(rims[1], rims[0], "inner")
    scale = 1.0 / math.sqrt(rows_dev * dom_size * lax.axis_size("inner"))
    state = reduce_grads(grads, gbias, scale)
    state, slots, low, high = lax.optimization_barrier((state, slots, low, high))
    returned = lax.all_to_all(slots, "dom", split_axis=0, concat_axis=0, tiled=True)
    sum_self, sum_neigh, sum_bias = gather_grads(state, width)
    grad_features = pl.pallas_call(
        combine_kernel,
        out_shape=jax.ShapeDtypeStruct(blocks.shape, BF16),
        in_specs=[SMEM] + [VMEM] * 4,
        out_specs=VMEM,
        scratch_shapes=[pltpu.VMEM(blocks.shape, F32)],
        compiler_params=params(),
        cost_estimate=pl.CostEstimate(
            flops=10**6, bytes_accessed=3 * 10**6, transcendentals=0
        ),
    )(send_blocks, own, returned, low, high)
    return (
        layer_out.reshape(rows_dev, width),
        grad_features.reshape(rows_dev, width),
        sum_self,
        sum_neigh,
        sum_bias.reshape(-1),
    )


def solution(mesh):
    return jax.shard_map(
        per_device,
        mesh=mesh,
        in_specs=(
            P(("dom", "inner"), None),
            P(("dom", "inner"), None, None, None),
            P(("dom", "inner"), None),
            P(("dom", "inner")),
            P(("dom", "inner"), None),
            P(),
            P(),
            P(),
            P(("dom", "inner"), None),
        ),
        out_specs=(P(("dom", "inner"), None), P(("dom", "inner"), None), P(), P(), P()),
        check_vma=False,
    )
```

```python
import functools
import math

import jax
import jax.numpy as jnp
from jax import lax
from jax.experimental import pallas as pl
from jax.experimental.pallas import tpu as pltpu
from jax.sharding import PartitionSpec as P

LANES = 128
VMEM = pl.BlockSpec(memory_space=pltpu.VMEM)
SMEM = pl.BlockSpec(memory_space=pltpu.SMEM)
ANY = pl.BlockSpec(memory_space=pl.ANY)
HBM = pl.BlockSpec(memory_space=pltpu.HBM)
F32 = jnp.float32
BF16 = jnp.bfloat16
CONTRACT_ROWS = (((0,), (0,)), ((), ()))
CONTRACT_COLS = (((1,), (1,)), ((), ()))


def params(mebibytes=32):
    return pltpu.CompilerParams(vmem_limit_bytes=mebibytes * 1024 * 1024)


def pick_kernel(send_ref, blocks_ref, out_ref, sems):
    copies = [
        pltpu.make_async_copy(blocks_ref.at[send_ref[0, j]], out_ref.at[j], sems.at[j])
        for j in range(out_ref.shape[0])
    ]
    for copy in copies:
        copy.start()
    for copy in copies:
        copy.wait()


def split_bias(bias):
    high = bias.astype(BF16).astype(F32)
    return [high, bias - high]


def piece_kernel(pieces_ref, gbias_ref, out_ref):
    summed = jnp.sum(pieces_ref[...].astype(F32), axis=0)
    hidden = summed.shape[1]
    lanes = [summed[:, k : k + LANES] for k in range(0, hidden, LANES)]
    bias = [gbias_ref[:, k : k + LANES] for k in range(0, hidden, LANES)]
    tail = split_bias(jnp.concatenate(bias, axis=0))
    tail.append(jnp.zeros((out_ref.shape[1] // 2 - 2 * len(bias), LANES), F32))
    piece = jnp.concatenate(lanes + tail, axis=0).astype(BF16)
    out_ref[...] = jnp.broadcast_to(piece[None], out_ref.shape)


def start_kernel(scale, spread_ref, out_ref):
    rows = out_ref.shape[1]
    bias_rows = 2
    summed = jnp.sum(spread_ref[...].astype(F32), axis=0) * scale
    out_ref[0] = summed[:rows].astype(BF16)
    tail = summed[rows:]
    bias = tail[:bias_rows] + tail[bias_rows : 2 * bias_rows]
    spare = jnp.zeros((rows - 2 * bias_rows, LANES), F32)
    out_ref[1] = jnp.concatenate(split_bias(bias) + [spare], axis=0).astype(BF16)


def grow_kernel(low, place_ref, mine_ref, *refs):
    theirs_refs, out_ref = refs[:-1], refs[-1]
    count = mine_ref.shape[0] - 1
    value = lax.bitwise_and(lax.shift_right_logical(place_ref[0], low), len(theirs_refs))
    out_ref[pl.ds(value * count, count)] = mine_ref[:count]
    tail = mine_ref[count].astype(F32)
    for mask, theirs_ref in enumerate(theirs_refs, 1):
        other = lax.bitwise_xor(value, mask)
        out_ref[pl.ds(other * count, count)] = theirs_ref[:count]
        tail = tail + theirs_ref[count].astype(F32)
    bias_rows = 2
    bias = tail[:bias_rows] + tail[bias_rows : 2 * bias_rows]
    spare = jnp.zeros((tail.shape[0] - 2 * bias_rows, LANES), F32)
    last = out_ref.shape[0] - 1
    out_ref[last] = jnp.concatenate(split_bias(bias) + [spare], axis=0).astype(BF16)


def tile_row(tiles, b):
    return jnp.concatenate([tiles[b, p] for p in range(tiles.shape[1])], axis=1)


def by_degree(values, inverse, b):
    rows = inverse.shape[1]
    return jnp.concatenate(
        [values[:, k : k + rows] * inverse[b] for k in range(0, values.shape[1], rows)], axis=1
    )


def invert_degree(degree_ref, inverse):
    for b in range(inverse.shape[0]):
        row = 1.0 / degree_ref[b : b + 1, :].astype(F32)
        inverse[b] = jnp.broadcast_to(row, inverse.shape[1:]).T


def forward_kernel(
    pairs_ref,
    degree_ref,
    w_self_ref,
    w_neigh_ref,
    bias_ref,
    blocks_hbm,
    left_ref,
    right_ref,
    received_hbm,
    tiles_hbm,
    cot_hbm,
    out_hbm,
    grad_hbm,
    grads_ref,
    gbias_ref,
    table,
    tiles,
    cot,
    out,
    sources,
    mean,
    grad_pre,
    inverse,
    sems,
    tile_sems,
):
    nblocks, npairs, rows, _ = tiles.shape
    width = table.shape[2]
    copies = [
        pltpu.make_async_copy(blocks_hbm, table.at[pl.ds(0, nblocks)], sems.at[0]),
        pltpu.make_async_copy(
            received_hbm, table.at[pl.ds(nblocks + 2, received_hbm.shape[0])], sems.at[1]
        ),
    ]
    tile_copies = [
        pltpu.make_async_copy(tiles_hbm.at[b], tiles.at[b], tile_sems.at[b])
        for b in range(nblocks)
    ]
    cot_copy = pltpu.make_async_copy(cot_hbm, cot, sems.at[2])
    out_copy = pltpu.make_async_copy(out, out_hbm, sems.at[3])
    grad_copy = pltpu.make_async_copy(grad_pre, grad_hbm, sems.at[4])
    for copy in copies:
        copy.start()
    for copy in tile_copies:
        copy.start()
    cot_copy.start()
    table[nblocks] = left_ref[...]
    table[nblocks + 1] = right_ref[...]
    invert_degree(degree_ref, inverse)
    for copy in copies:
        copy.wait()

    cot_copy.wait()
    w_self = w_self_ref[...]
    w_neigh = w_neigh_ref[...]
    gbias = jnp.zeros((1, width), F32)
    def aggregate(b):
        for p in range(npairs):
            sources[b % 2, pl.ds(p * rows, rows), :] = table[pairs_ref[b, p]]
        stacked = sources[b % 2]
        tile_copies[b].wait()
        summed = jnp.dot(tile_row(tiles, b), stacked, preferred_element_type=F32)
        mean[b] = by_degree(summed, inverse, b).astype(BF16)

    def activate(b, gbias):
        features = table[b : b + step].reshape(step * rows, width)
        means = mean[b : b + step].reshape(step * rows, width)
        preact = (
            jnp.dot(features, w_self, preferred_element_type=F32)
            + jnp.dot(means, w_neigh, preferred_element_type=F32)
            + bias_ref[...]
        )
        sigma = jax.nn.sigmoid(preact)
        out[b : b + step] = (preact * sigma).astype(BF16).reshape(step, rows, width)
        cots = cot[b : b + step].reshape(step * rows, width).astype(F32)
        grad = (cots * sigma * (1.0 + preact * (1.0 - sigma))).astype(BF16)
        grad_pre[pl.ds(b * rows, step * rows), :] = grad
        return gbias + jnp.sum(grad.astype(F32), axis=0, keepdims=True)

    step = 2
    for b in range(nblocks):
        aggregate(b)
    for b in range(0, nblocks, step):
        gbias = activate(b, gbias)
    grad_copy.start()
    out_copy.start()
    gbias_ref[...] = gbias

    grads = grad_pre[...]
    features = table[:nblocks].reshape(nblocks * rows, width)
    means = mean[...].reshape(nblocks * rows, width)
    grads_ref[:width, :] = lax.dot_general(
        features, grads, CONTRACT_ROWS, preferred_element_type=F32
    ).astype(BF16)
    grads_ref[width:, :] = lax.dot_general(
        means, grads, CONTRACT_ROWS, preferred_element_type=F32
    ).astype(BF16)
    grad_copy.wait()
    out_copy.wait()


def backward_kernel(
    pairs_ref,
    degree_ref,
    w_self_ref,
    w_neigh_ref,
    grad_ref,
    tiles_hbm,
    own_ref,
    rims_ref,
    slots_ref,
    tiles,
    inverse,
    entries,
    tile_sems,
):
    nblocks, npairs, rows, _ = tiles.shape
    width = w_self_ref.shape[0]
    tile_copies = [
        pltpu.make_async_copy(tiles_hbm.at[b], tiles.at[b], tile_sems.at[b])
        for b in range(nblocks)
    ]
    for copy in tile_copies:
        copy.start()
    invert_degree(degree_ref, inverse)
    entries[nblocks:] = jnp.zeros((entries.shape[0] - nblocks, rows, width), F32)
    w_self = w_self_ref[...]
    w_neigh = w_neigh_ref[...]
    own = lax.dot_general(grad_ref[...], w_self, CONTRACT_COLS, preferred_element_type=F32)
    entries[:nblocks] = own.reshape(nblocks, rows, width)
    for b in range(nblocks):
        grad = grad_ref[pl.ds(b * rows, rows), :]
        grad_mean = lax.dot_general(grad, w_neigh, CONTRACT_COLS, preferred_element_type=F32)
        grad_mean = by_degree(grad_mean, inverse, b).astype(BF16)
        tile_copies[b].wait()
        parts = lax.dot_general(
            tile_row(tiles, b), grad_mean, CONTRACT_ROWS, preferred_element_type=F32
        )
        for p in range(npairs):
            entry = pairs_ref[b, p]
            entries[entry] = entries[entry] + parts[p * rows : (p + 1) * rows]

    own_ref[...] = entries[:nblocks]
    rims_ref[...] = entries[nblocks : nblocks + 2].astype(BF16)
    slots_ref[...] = entries[nblocks + 2 :].astype(BF16)


def combine_kernel(send_ref, own_ref, returned_ref, low_ref, high_ref, out_ref, total):
    total[...] = own_ref[...]
    last = total.shape[0] - 1
    total[0] = total[0] + low_ref[...].astype(F32)
    total[last] = total[last] + high_ref[...].astype(F32)
    for j in range(returned_ref.shape[0]):
        block = send_ref[0, j]
        total[block] = total[block] + returned_ref[j].astype(F32)
    out_ref[...] = total[...].astype(BF16)


def call_forward(
    blocks, left, right, received, tiles, cot, pairs, degree, w_self, w_neigh, bias
):
    nblocks, npairs, rows, _ = tiles.shape
    width = blocks.shape[2]
    entries = nblocks + 2 + received.shape[0]
    shape = jax.ShapeDtypeStruct
    return pl.pallas_call(
        forward_kernel,
        out_shape=(
            shape(blocks.shape, BF16),
            shape((nblocks * rows, width), BF16),
            shape((2 * width, width), BF16),
            shape((1, width), F32),
        ),
        in_specs=[SMEM] + [VMEM] * 4 + [HBM, VMEM, VMEM, HBM, HBM, HBM],
        out_specs=(ANY, ANY, VMEM, VMEM),
        scratch_shapes=[
            pltpu.VMEM((entries, rows, width), BF16),
            pltpu.VMEM(tiles.shape, BF16),
            pltpu.VMEM(blocks.shape, BF16),
            pltpu.VMEM(blocks.shape, BF16),
            pltpu.VMEM((2, npairs * rows, width), BF16),
            pltpu.VMEM(blocks.shape, BF16),
            pltpu.VMEM((nblocks * rows, width), BF16),
            pltpu.VMEM((nblocks, rows, rows), F32),
            pltpu.SemaphoreType.DMA((5,)),
            pltpu.SemaphoreType.DMA((nblocks,)),
        ],
        compiler_params=params(58),
        cost_estimate=pl.CostEstimate(
            flops=2 * 10**9, bytes_accessed=6 * 10**6, transcendentals=nblocks * rows * width
        ),
    )(pairs, degree, w_self, w_neigh, bias, blocks, left, right, received, tiles, cot)


def call_backward(grad, tiles, pairs, degree, w_self, w_neigh):
    nblocks, _, rows, _ = tiles.shape
    width = w_self.shape[0]
    dom = lax.axis_size("dom")
    shape = jax.ShapeDtypeStruct
    return pl.pallas_call(
        backward_kernel,
        out_shape=(
            shape((nblocks, rows, width), F32),
            shape((2, rows, width), BF16),
            shape((dom, rows, width), BF16),
        ),
        in_specs=[SMEM] + [VMEM] * 4 + [HBM],
        out_specs=(VMEM,) * 3,
        scratch_shapes=[
            pltpu.VMEM(tiles.shape, BF16),
            pltpu.VMEM((nblocks, rows, rows), F32),
            pltpu.VMEM((nblocks + 2 + dom, rows, width), F32),
            pltpu.SemaphoreType.DMA((nblocks,)),
        ],
        compiler_params=params(58),
        cost_estimate=pl.CostEstimate(
            flops=2 * 10**9, bytes_accessed=8 * 10**6, transcendentals=0
        ),
    )(pairs, degree, w_self, w_neigh, grad, tiles)


def neighbours(low_source, high_source, axis):
    count = lax.axis_size(axis)
    forward = [(i, i + 1) for i in range(count - 1)]
    backward = [(target, source) for source, target in forward]
    return lax.ppermute(low_source, axis, forward), lax.ppermute(high_source, axis, backward)


def reduce_grads(grads, gbias, scale):
    dom_size = lax.axis_size("dom")
    inner_size = lax.axis_size("inner")
    hidden = grads.shape[1]
    chunks = grads.reshape(inner_size, grads.shape[0] // inner_size, hidden)
    pieces = lax.all_to_all(chunks, "inner", split_axis=0, concat_axis=0, tiled=True)
    rows = chunks.shape[1] * chunks.shape[2] // LANES
    spread = pl.pallas_call(
        piece_kernel,
        out_shape=jax.ShapeDtypeStruct((dom_size, 2 * rows, LANES), BF16),
        in_specs=[VMEM, VMEM],
        out_specs=VMEM,
        compiler_params=params(),
    )(pieces, gbias)
    spread = lax.all_to_all(spread, "dom", split_axis=0, concat_axis=0, tiled=True)
    return pl.pallas_call(
        functools.partial(start_kernel, scale),
        out_shape=jax.ShapeDtypeStruct((2, rows, LANES), BF16),
        in_specs=[VMEM],
        out_specs=VMEM,
        compiler_params=params(),
    )(spread)


def gather_grads(state, hidden, beside):
    inner_size = lax.axis_size("inner")
    bits = inner_size.bit_length() - 1
    groups = [(low, 1) for low in reversed(range(bits))]
    index = lax.axis_index("inner").astype(jnp.int32).reshape(1)
    place = [0] * inner_size
    for low, size in groups:
        count = state.shape[0] - 1
        theirs = []
        for mask in range(1, 1 << size):
            pairs = [(i, i ^ (mask << low)) for i in range(inner_size)]
            theirs.append(lax.ppermute(state, "inner", pairs))
        if low == groups[-1][0]:
            theirs, beside = lax.optimization_barrier((theirs, beside))
        place = [
            where + ((chunk >> low) % (1 << size)) * count for chunk, where in enumerate(place)
        ]
        state = pl.pallas_call(
            functools.partial(grow_kernel, low),
            out_shape=jax.ShapeDtypeStruct(((count << size) + 1,) + state.shape[1:], BF16),
            in_specs=[SMEM] + [VMEM] * (1 + len(theirs)),
            out_specs=VMEM,
            compiler_params=params(),
        )(index, state, *theirs)
    unpacked = pl.pallas_call(
        functools.partial(unpack_kernel, place),
        out_shape=(
            jax.ShapeDtypeStruct((hidden, hidden), F32),
            jax.ShapeDtypeStruct((hidden, hidden), F32),
            jax.ShapeDtypeStruct((2, LANES), F32),
        ),
        in_specs=[VMEM],
        out_specs=(VMEM,) * 3,
        compiler_params=params(),
    )(state)
    return unpacked, beside


def unpack_kernel(place, state_ref, self_ref, neigh_ref, bias_ref):
    hidden = self_ref.shape[1]
    groups = hidden // LANES
    rows = state_ref.shape[1] // groups
    half = len(place) // 2
    for chunk, where in enumerate(place):
        ref = self_ref if chunk < half else neigh_ref
        first = (chunk % half) * rows
        values = state_ref[where].astype(F32)
        for k in range(groups):
            ref[first : first + rows, k * LANES : (k + 1) * LANES] = values[
                k * rows : (k + 1) * rows
            ]
    tail = state_ref[len(place)].astype(F32)
    bias_ref[...] = tail[:groups] + tail[groups : 2 * groups]


def per_device(
    features, tiles, pair_source, in_degree, send_blocks, w_self, w_neigh, bias, cotangent
):
    rows_dev, width = features.shape
    nblocks, _, rows, _ = tiles.shape
    dom_size = lax.axis_size("dom")
    blocks = features.reshape(nblocks, rows, width)
    outgoing = pl.pallas_call(
        pick_kernel,
        out_shape=jax.ShapeDtypeStruct((dom_size, rows, width), BF16),
        in_specs=[SMEM, HBM],
        out_specs=VMEM,
        scratch_shapes=[pltpu.SemaphoreType.DMA((dom_size,))],
        compiler_params=params(58),
    )(send_blocks, blocks)
    received = lax.all_to_all(outgoing, "dom", split_axis=0, concat_axis=0, tiled=True)
    left, right = neighbours(blocks[nblocks - 1], blocks[0], "inner")
    degree = in_degree.reshape(nblocks, rows)
    layer_out, grad_pre, grads, gbias = call_forward(
        blocks,
        left,
        right,
        received,
        tiles,
        cotangent.reshape(nblocks, rows, width),
        pair_source,
        degree,
        w_self,
        w_neigh,
        bias[None, :],
    )
    own, rims, slots = call_backward(grad_pre, tiles, pair_source, degree, w_self, w_neigh)
    low, high = neighbours(rims[1], rims[0], "inner")
    scale = 1.0 / math.sqrt(rows_dev * dom_size * lax.axis_size("inner"))
    state = reduce_grads(grads, gbias, scale)
    state, slots, low, high = lax.optimization_barrier((state, slots, low, high))
    returned = lax.all_to_all(slots, "dom", split_axis=0, concat_axis=0, tiled=True)
    grad_features = pl.pallas_call(
        combine_kernel,
        out_shape=jax.ShapeDtypeStruct(blocks.shape, BF16),
        in_specs=[SMEM] + [VMEM] * 4,
        out_specs=VMEM,
        scratch_shapes=[pltpu.VMEM(blocks.shape, F32)],
        compiler_params=params(),
        cost_estimate=pl.CostEstimate(
            flops=10**6, bytes_accessed=3 * 10**6, transcendentals=0
        ),
    )(send_blocks, own, returned, low, high)
    (sum_self, sum_neigh, sum_bias), grad_features = gather_grads(state, width, grad_features)
    return (
        layer_out.reshape(rows_dev, width),
        grad_features.reshape(rows_dev, width),
        sum_self,
        sum_neigh,
        sum_bias.reshape(-1),
    )


def solution(mesh):
    return jax.shard_map(
        per_device,
        mesh=mesh,
        in_specs=(
            P(("dom", "inner"), None),
            P(("dom", "inner"), None, None, None),
            P(("dom", "inner"), None),
            P(("dom", "inner")),
            P(("dom", "inner"), None),
            P(),
            P(),
            P(),
            P(("dom", "inner"), None),
        ),
        out_specs=(P(("dom", "inner"), None), P(("dom", "inner"), None), P(), P(), P()),
        check_vma=False,
    )
```

```python
import functools
import math

import jax
import jax.numpy as jnp
from jax import lax
from jax.experimental import pallas as pl
from jax.experimental.pallas import tpu as pltpu
from jax.sharding import Mesh
from jax.sharding import PartitionSpec as P

LANES = 128
INNER = ("hi", "mid", "lo")
ALL = ("dom",) + INNER
VMEM = pl.BlockSpec(memory_space=pltpu.VMEM)
SMEM = pl.BlockSpec(memory_space=pltpu.SMEM)
ANY = pl.BlockSpec(memory_space=pl.ANY)
HBM = pl.BlockSpec(memory_space=pltpu.HBM)
F32 = jnp.float32
BF16 = jnp.bfloat16
CONTRACT_ROWS = (((0,), (0,)), ((), ()))
CONTRACT_COLS = (((1,), (1,)), ((), ()))


def params(mebibytes=32):
    return pltpu.CompilerParams(vmem_limit_bytes=mebibytes * 1024 * 1024)


def pick_kernel(send_ref, blocks_ref, out_ref, sems):
    copies = [
        pltpu.make_async_copy(blocks_ref.at[send_ref[0, j]], out_ref.at[j], sems.at[j])
        for j in range(out_ref.shape[0])
    ]
    for copy in copies:
        copy.start()
    for copy in copies:
        copy.wait()


def split_bias(bias):
    high = bias.astype(BF16).astype(F32)
    return [high, bias - high]


def piece_kernel(pieces_ref, gbias_ref, out_ref):
    summed = jnp.sum(pieces_ref[...].astype(F32), axis=0)
    hidden = summed.shape[1]
    lanes = [summed[:, k : k + LANES] for k in range(0, hidden, LANES)]
    bias = [gbias_ref[:, k : k + LANES] for k in range(0, hidden, LANES)]
    tail = split_bias(jnp.concatenate(bias, axis=0))
    tail.append(jnp.zeros((8 - 2 * len(bias), LANES), F32))
    piece = jnp.concatenate(lanes + tail, axis=0).astype(BF16)
    out_ref[...] = jnp.broadcast_to(piece[None], out_ref.shape)


def start_kernel(scale, spread_ref, out_ref):
    count, rows = out_ref.shape[0] - 1, out_ref.shape[1]
    bias_rows = 2
    spread = spread_ref[...].astype(F32)
    spread = spread.reshape((spread.shape[0] // count, count) + spread.shape[1:])
    summed = jnp.sum(spread, axis=0) * scale
    out_ref[:count] = summed[:, :rows].astype(BF16)
    tail = jnp.sum(summed[:, rows:], axis=0)
    bias = tail[:bias_rows] + tail[bias_rows : 2 * bias_rows]
    spare = jnp.zeros((rows - 2 * bias_rows, LANES), F32)
    out_ref[count] = jnp.concatenate(split_bias(bias) + [spare], axis=0).astype(BF16)


def grow_kernel(low, place_ref, mine_ref, *refs):
    theirs_refs, out_ref = refs[:-1], refs[-1]
    count = mine_ref.shape[0] - 1
    value = lax.bitwise_and(lax.shift_right_logical(place_ref[0], low), len(theirs_refs))
    out_ref[pl.ds(value * count, count)] = mine_ref[:count]
    tail = mine_ref[count].astype(F32)
    for mask, theirs_ref in enumerate(theirs_refs, 1):
        other = lax.bitwise_xor(value, mask)
        out_ref[pl.ds(other * count, count)] = theirs_ref[:count]
        tail = tail + theirs_ref[count].astype(F32)
    bias_rows = 2
    bias = tail[:bias_rows] + tail[bias_rows : 2 * bias_rows]
    spare = jnp.zeros((tail.shape[0] - 2 * bias_rows, LANES), F32)
    last = out_ref.shape[0] - 1
    out_ref[last] = jnp.concatenate(split_bias(bias) + [spare], axis=0).astype(BF16)


def tile_row(tiles, b):
    return jnp.concatenate([tiles[b, p] for p in range(tiles.shape[1])], axis=1)


def by_degree(values, inverse, b):
    rows = inverse.shape[1]
    return jnp.concatenate(
        [values[:, k : k + rows] * inverse[b] for k in range(0, values.shape[1], rows)], axis=1
    )


def invert_degree(degree_ref, inverse):
    for b in range(inverse.shape[0]):
        row = 1.0 / degree_ref[b : b + 1, :].astype(F32)
        inverse[b] = jnp.broadcast_to(row, inverse.shape[1:]).T


def forward_kernel(
    pairs_ref,
    degree_ref,
    w_self_ref,
    w_neigh_ref,
    bias_ref,
    blocks_hbm,
    left_ref,
    right_ref,
    received_hbm,
    tiles_hbm,
    cot_hbm,
    out_hbm,
    grad_hbm,
    grads_ref,
    gbias_ref,
    table,
    tiles,
    cot,
    out,
    sources,
    mean,
    grad_pre,
    inverse,
    sems,
    tile_sems,
):
    nblocks, npairs, rows, _ = tiles.shape
    width = table.shape[2]
    copies = [
        pltpu.make_async_copy(blocks_hbm, table.at[pl.ds(0, nblocks)], sems.at[0]),
        pltpu.make_async_copy(
            received_hbm, table.at[pl.ds(nblocks + 2, received_hbm.shape[0])], sems.at[1]
        ),
    ]
    tile_copies = [
        pltpu.make_async_copy(tiles_hbm.at[b], tiles.at[b], tile_sems.at[b])
        for b in range(nblocks)
    ]
    cot_copy = pltpu.make_async_copy(cot_hbm, cot, sems.at[2])
    out_copy = pltpu.make_async_copy(out, out_hbm, sems.at[3])
    grad_copy = pltpu.make_async_copy(grad_pre, grad_hbm, sems.at[4])
    for copy in copies:
        copy.start()
    for copy in tile_copies:
        copy.start()
    cot_copy.start()
    table[nblocks] = left_ref[...]
    table[nblocks + 1] = right_ref[...]
    invert_degree(degree_ref, inverse)
    for copy in copies:
        copy.wait()

    cot_copy.wait()
    w_self = w_self_ref[...]
    w_neigh = w_neigh_ref[...]
    gbias = jnp.zeros((1, width), F32)
    def aggregate(b):
        for p in range(npairs):
            sources[b % 2, pl.ds(p * rows, rows), :] = table[pairs_ref[b, p]]
        stacked = sources[b % 2]
        tile_copies[b].wait()
        summed = jnp.dot(tile_row(tiles, b), stacked, preferred_element_type=F32)
        mean[b] = by_degree(summed, inverse, b).astype(BF16)

    def activate(b, gbias):
        features = table[b : b + step].reshape(step * rows, width)
        means = mean[b : b + step].reshape(step * rows, width)
        preact = (
            jnp.dot(features, w_self, preferred_element_type=F32)
            + jnp.dot(means, w_neigh, preferred_element_type=F32)
            + bias_ref[...]
        )
        sigma = jax.nn.sigmoid(preact)
        out[b : b + step] = (preact * sigma).astype(BF16).reshape(step, rows, width)
        cots = cot[b : b + step].reshape(step * rows, width).astype(F32)
        grad = (cots * sigma * (1.0 + preact * (1.0 - sigma))).astype(BF16)
        grad_pre[pl.ds(b * rows, step * rows), :] = grad
        return gbias + jnp.sum(grad.astype(F32), axis=0, keepdims=True)

    step = 2
    for b in range(nblocks):
        aggregate(b)
    for b in range(0, nblocks, step):
        gbias = activate(b, gbias)
    grad_copy.start()
    out_copy.start()
    gbias_ref[...] = gbias

    grads = grad_pre[...]
    features = table[:nblocks].reshape(nblocks * rows, width)
    means = mean[...].reshape(nblocks * rows, width)
    grads_ref[:width, :] = lax.dot_general(
        features, grads, CONTRACT_ROWS, preferred_element_type=F32
    ).astype(BF16)
    grads_ref[width:, :] = lax.dot_general(
        means, grads, CONTRACT_ROWS, preferred_element_type=F32
    ).astype(BF16)
    grad_copy.wait()
    out_copy.wait()


def backward_kernel(
    pairs_ref,
    degree_ref,
    w_self_ref,
    w_neigh_ref,
    grad_ref,
    tiles_hbm,
    own_ref,
    rims_ref,
    slots_ref,
    tiles,
    inverse,
    entries,
    tile_sems,
):
    nblocks, npairs, rows, _ = tiles.shape
    width = w_self_ref.shape[0]
    tile_copies = [
        pltpu.make_async_copy(tiles_hbm.at[b], tiles.at[b], tile_sems.at[b])
        for b in range(nblocks)
    ]
    for copy in tile_copies:
        copy.start()
    invert_degree(degree_ref, inverse)
    entries[nblocks:] = jnp.zeros((entries.shape[0] - nblocks, rows, width), F32)
    w_self = w_self_ref[...]
    w_neigh = w_neigh_ref[...]
    own = lax.dot_general(grad_ref[...], w_self, CONTRACT_COLS, preferred_element_type=F32)
    entries[:nblocks] = own.reshape(nblocks, rows, width)
    for b in range(nblocks):
        grad = grad_ref[pl.ds(b * rows, rows), :]
        grad_mean = lax.dot_general(grad, w_neigh, CONTRACT_COLS, preferred_element_type=F32)
        grad_mean = by_degree(grad_mean, inverse, b).astype(BF16)
        tile_copies[b].wait()
        parts = lax.dot_general(
            tile_row(tiles, b), grad_mean, CONTRACT_ROWS, preferred_element_type=F32
        )
        for p in range(npairs):
            entry = pairs_ref[b, p]
            entries[entry] = entries[entry] + parts[p * rows : (p + 1) * rows]

    own_ref[...] = entries[:nblocks]
    rims_ref[...] = entries[nblocks : nblocks + 2].astype(BF16)
    slots_ref[...] = entries[nblocks + 2 :].astype(BF16)


def combine_kernel(send_ref, own_ref, returned_ref, low_ref, high_ref, out_ref, total):
    total[...] = own_ref[...]
    last = total.shape[0] - 1
    total[0] = total[0] + low_ref[...].astype(F32)
    total[last] = total[last] + high_ref[...].astype(F32)
    for j in range(returned_ref.shape[0]):
        block = send_ref[0, j]
        total[block] = total[block] + returned_ref[j].astype(F32)
    out_ref[...] = total[...].astype(BF16)


def call_forward(
    blocks, left, right, received, tiles, cot, pairs, degree, w_self, w_neigh, bias
):
    nblocks, npairs, rows, _ = tiles.shape
    width = blocks.shape[2]
    entries = nblocks + 2 + received.shape[0]
    shape = jax.ShapeDtypeStruct
    return pl.pallas_call(
        forward_kernel,
        out_shape=(
            shape(blocks.shape, BF16),
            shape((nblocks * rows, width), BF16),
            shape((2 * width, width), BF16),
            shape((1, width), F32),
        ),
        in_specs=[SMEM] + [VMEM] * 4 + [HBM, VMEM, VMEM, HBM, HBM, HBM],
        out_specs=(ANY, ANY, VMEM, VMEM),
        scratch_shapes=[
            pltpu.VMEM((entries, rows, width), BF16),
            pltpu.VMEM(tiles.shape, BF16),
            pltpu.VMEM(blocks.shape, BF16),
            pltpu.VMEM(blocks.shape, BF16),
            pltpu.VMEM((2, npairs * rows, width), BF16),
            pltpu.VMEM(blocks.shape, BF16),
            pltpu.VMEM((nblocks * rows, width), BF16),
            pltpu.VMEM((nblocks, rows, rows), F32),
            pltpu.SemaphoreType.DMA((5,)),
            pltpu.SemaphoreType.DMA((nblocks,)),
        ],
        compiler_params=params(58),
        cost_estimate=pl.CostEstimate(
            flops=2 * 10**9, bytes_accessed=6 * 10**6, transcendentals=nblocks * rows * width
        ),
    )(pairs, degree, w_self, w_neigh, bias, blocks, left, right, received, tiles, cot)


def call_backward(grad, tiles, pairs, degree, w_self, w_neigh):
    nblocks, _, rows, _ = tiles.shape
    width = w_self.shape[0]
    dom = lax.axis_size("dom")
    shape = jax.ShapeDtypeStruct
    return pl.pallas_call(
        backward_kernel,
        out_shape=(
            shape((nblocks, rows, width), F32),
            shape((2, rows, width), BF16),
            shape((dom, rows, width), BF16),
        ),
        in_specs=[SMEM] + [VMEM] * 4 + [HBM],
        out_specs=(VMEM,) * 3,
        scratch_shapes=[
            pltpu.VMEM(tiles.shape, BF16),
            pltpu.VMEM((nblocks, rows, rows), F32),
            pltpu.VMEM((nblocks + 2 + dom, rows, width), F32),
            pltpu.SemaphoreType.DMA((nblocks,)),
        ],
        compiler_params=params(58),
        cost_estimate=pl.CostEstimate(
            flops=2 * 10**9, bytes_accessed=8 * 10**6, transcendentals=0
        ),
    )(pairs, degree, w_self, w_neigh, grad, tiles)


def neighbours(low_source, high_source, axis):
    count = lax.axis_size(axis)
    forward = [(i, i + 1) for i in range(count - 1)]
    backward = [(target, source) for source, target in forward]
    return lax.ppermute(low_source, axis, forward), lax.ppermute(high_source, axis, backward)


def reduce_grads(grads, gbias, scale):
    twins = lax.axis_size("mid")
    peers = lax.axis_size("dom") * twins
    inner_size = lax.axis_size(INNER)
    hidden = grads.shape[1]
    chunks = grads.reshape(inner_size, grads.shape[0] // inner_size, hidden)
    pieces = lax.all_to_all(chunks, INNER, split_axis=0, concat_axis=0, tiled=True)
    rows = chunks.shape[1] * chunks.shape[2] // LANES
    spread = pl.pallas_call(
        piece_kernel,
        out_shape=jax.ShapeDtypeStruct((peers, rows + 8, LANES), BF16),
        in_specs=[VMEM, VMEM],
        out_specs=VMEM,
        compiler_params=params(),
    )(pieces, gbias)
    spread = lax.all_to_all(spread, ("dom", "mid"), split_axis=0, concat_axis=0, tiled=True)
    return pl.pallas_call(
        functools.partial(start_kernel, scale),
        out_shape=jax.ShapeDtypeStruct((twins + 1, rows, LANES), BF16),
        in_specs=[VMEM],
        out_specs=VMEM,
        compiler_params=params(),
    )(spread)


def gather_grads(state, hidden, beside):
    inner_size = lax.axis_size(INNER)
    bits = inner_size.bit_length() - 1
    groups = [(low, 1) for low in reversed(range(bits)) if low != 1]
    index = lax.axis_index(INNER).astype(jnp.int32).reshape(1)
    place = [(chunk >> 1) % 2 for chunk in range(inner_size)]
    for low, size in groups:
        count = state.shape[0] - 1
        theirs = []
        for mask in range(1, 1 << size):
            pairs = [(i, i ^ (mask << low)) for i in range(inner_size)]
            theirs.append(lax.ppermute(state, INNER, pairs))
        if low == groups[-1][0]:
            theirs, beside = lax.optimization_barrier((theirs, beside))
        place = [
            where + ((chunk >> low) % (1 << size)) * count for chunk, where in enumerate(place)
        ]
        state = pl.pallas_call(
            functools.partial(grow_kernel, low),
            out_shape=jax.ShapeDtypeStruct(((count << size) + 1,) + state.shape[1:], BF16),
            in_specs=[SMEM] + [VMEM] * (1 + len(theirs)),
            out_specs=VMEM,
            compiler_params=params(),
        )(index, state, *theirs)
    unpacked = pl.pallas_call(
        functools.partial(unpack_kernel, place),
        out_shape=(
            jax.ShapeDtypeStruct((hidden, hidden), F32),
            jax.ShapeDtypeStruct((hidden, hidden), F32),
            jax.ShapeDtypeStruct((2, LANES), F32),
        ),
        in_specs=[VMEM],
        out_specs=(VMEM,) * 3,
        compiler_params=params(),
    )(state)
    return unpacked, beside


def unpack_kernel(place, state_ref, self_ref, neigh_ref, bias_ref):
    hidden = self_ref.shape[1]
    groups = hidden // LANES
    rows = state_ref.shape[1] // groups
    half = len(place) // 2
    for chunk, where in enumerate(place):
        ref = self_ref if chunk < half else neigh_ref
        first = (chunk % half) * rows
        values = state_ref[where].astype(F32)
        for k in range(groups):
            ref[first : first + rows, k * LANES : (k + 1) * LANES] = values[
                k * rows : (k + 1) * rows
            ]
    tail = state_ref[len(place)].astype(F32)
    bias_ref[...] = tail[:groups] + tail[groups : 2 * groups]


def per_device(
    features, tiles, pair_source, in_degree, send_blocks, w_self, w_neigh, bias, cotangent
):
    rows_dev, width = features.shape
    nblocks, _, rows, _ = tiles.shape
    dom_size = lax.axis_size("dom")
    blocks = features.reshape(nblocks, rows, width)
    outgoing = pl.pallas_call(
        pick_kernel,
        out_shape=jax.ShapeDtypeStruct((dom_size, rows, width), BF16),
        in_specs=[SMEM, HBM],
        out_specs=VMEM,
        scratch_shapes=[pltpu.SemaphoreType.DMA((dom_size,))],
        compiler_params=params(58),
    )(send_blocks, blocks)
    received = lax.all_to_all(outgoing, "dom", split_axis=0, concat_axis=0, tiled=True)
    left, right = neighbours(blocks[nblocks - 1], blocks[0], INNER)
    degree = in_degree.reshape(nblocks, rows)
    layer_out, grad_pre, grads, gbias = call_forward(
        blocks,
        left,
        right,
        received,
        tiles,
        cotangent.reshape(nblocks, rows, width),
        pair_source,
        degree,
        w_self,
        w_neigh,
        bias[None, :],
    )
    own, rims, slots = call_backward(grad_pre, tiles, pair_source, degree, w_self, w_neigh)
    low, high = neighbours(rims[1], rims[0], INNER)
    scale = 1.0 / math.sqrt(rows_dev * dom_size * lax.axis_size(INNER))
    state = reduce_grads(grads, gbias, scale)
    state, slots, low, high = lax.optimization_barrier((state, slots, low, high))
    returned = lax.all_to_all(slots, "dom", split_axis=0, concat_axis=0, tiled=True)
    grad_features = pl.pallas_call(
        combine_kernel,
        out_shape=jax.ShapeDtypeStruct(blocks.shape, BF16),
        in_specs=[SMEM] + [VMEM] * 4,
        out_specs=VMEM,
        scratch_shapes=[pltpu.VMEM(blocks.shape, F32)],
        compiler_params=params(),
        cost_estimate=pl.CostEstimate(
            flops=10**6, bytes_accessed=3 * 10**6, transcendentals=0
        ),
    )(send_blocks, own, returned, low, high)
    (sum_self, sum_neigh, sum_bias), grad_features = gather_grads(state, width, grad_features)
    return (
        layer_out.reshape(rows_dev, width),
        grad_features.reshape(rows_dev, width),
        sum_self,
        sum_neigh,
        sum_bias.reshape(-1),
    )


def solution(mesh):
    devices = mesh.devices.reshape(mesh.shape["dom"], -1, 2, 2)
    return jax.shard_map(
        per_device,
        mesh=Mesh(devices, ALL),
        in_specs=(
            P(ALL, None),
            P(ALL, None, None, None),
            P(ALL, None),
            P(ALL),
            P(ALL, None),
            P(),
            P(),
            P(),
            P(ALL, None),
        ),
        out_specs=(P(ALL, None), P(ALL, None), P(), P(), P()),
        check_vma=False,
    )
```

```python
import functools
import math

import jax
import jax.numpy as jnp
from jax import lax
from jax.experimental import pallas as pl
from jax.experimental.pallas import tpu as pltpu
from jax.sharding import Mesh
from jax.sharding import PartitionSpec as P

LANES = 128
INNER = ("hi", "mid", "lo")
ALL = ("dom",) + INNER
VMEM = pl.BlockSpec(memory_space=pltpu.VMEM)
SMEM = pl.BlockSpec(memory_space=pltpu.SMEM)
ANY = pl.BlockSpec(memory_space=pl.ANY)
HBM = pl.BlockSpec(memory_space=pltpu.HBM)
F32 = jnp.float32
BF16 = jnp.bfloat16
CONTRACT_ROWS = (((0,), (0,)), ((), ()))
CONTRACT_COLS = (((1,), (1,)), ((), ()))


def params(mebibytes=32):
    return pltpu.CompilerParams(vmem_limit_bytes=mebibytes * 1024 * 1024)


def pick_kernel(send_ref, blocks_ref, out_ref, sems):
    copies = [
        pltpu.make_async_copy(blocks_ref.at[send_ref[0, j]], out_ref.at[j], sems.at[j])
        for j in range(out_ref.shape[0])
    ]
    for copy in copies:
        copy.start()
    for copy in copies:
        copy.wait()


def split_bias(bias):
    high = bias.astype(BF16).astype(F32)
    return [high, bias - high]


def piece_kernel(pieces_ref, gbias_ref, out_ref):
    summed = jnp.sum(pieces_ref[...].astype(F32), axis=0)
    hidden = summed.shape[1]
    lanes = [summed[:, k : k + LANES] for k in range(0, hidden, LANES)]
    bias = [gbias_ref[:, k : k + LANES] for k in range(0, hidden, LANES)]
    tail = split_bias(jnp.concatenate(bias, axis=0))
    tail.append(jnp.zeros((8 - 2 * len(bias), LANES), F32))
    piece = jnp.concatenate(lanes + tail, axis=0).astype(BF16)
    out_ref[...] = jnp.broadcast_to(piece[None], out_ref.shape)


def start_kernel(scale, spread_ref, out_ref):
    count, rows = out_ref.shape[0] - 1, out_ref.shape[1]
    bias_rows = 2
    spread = spread_ref[...].astype(F32)
    spread = spread.reshape((spread.shape[0] // count, count) + spread.shape[1:])
    summed = jnp.sum(spread, axis=0) * scale
    out_ref[:count] = summed[:, :rows].astype(BF16)
    tail = jnp.sum(summed[:, rows:], axis=0)
    bias = tail[:bias_rows] + tail[bias_rows : 2 * bias_rows]
    spare = jnp.zeros((rows - 2 * bias_rows, LANES), F32)
    out_ref[count] = jnp.concatenate(split_bias(bias) + [spare], axis=0).astype(BF16)


def grow_kernel(low, place_ref, mine_ref, *refs):
    theirs_refs, out_ref = refs[:-1], refs[-1]
    count = mine_ref.shape[0] - 1
    value = lax.bitwise_and(lax.shift_right_logical(place_ref[0], low), len(theirs_refs))
    out_ref[pl.ds(value * count, count)] = mine_ref[:count]
    tail = mine_ref[count].astype(F32)
    for mask, theirs_ref in enumerate(theirs_refs, 1):
        other = lax.bitwise_xor(value, mask)
        out_ref[pl.ds(other * count, count)] = theirs_ref[:count]
        tail = tail + theirs_ref[count].astype(F32)
    bias_rows = 2
    bias = tail[:bias_rows] + tail[bias_rows : 2 * bias_rows]
    spare = jnp.zeros((tail.shape[0] - 2 * bias_rows, LANES), F32)
    last = out_ref.shape[0] - 1
    out_ref[last] = jnp.concatenate(split_bias(bias) + [spare], axis=0).astype(BF16)


def tile_row(tiles, b):
    return jnp.concatenate([tiles[b, p] for p in range(tiles.shape[1])], axis=1)


def by_degree(values, inverse, b):
    rows = inverse.shape[1]
    return jnp.concatenate(
        [values[:, k : k + rows] * inverse[b] for k in range(0, values.shape[1], rows)], axis=1
    )


def invert_degree(degree_ref, inverse):
    for b in range(inverse.shape[0]):
        row = 1.0 / degree_ref[b : b + 1, :].astype(F32)
        inverse[b] = jnp.broadcast_to(row, inverse.shape[1:]).T


def forward_kernel(
    pairs_ref,
    degree_ref,
    w_self_ref,
    w_neigh_ref,
    bias_ref,
    blocks_hbm,
    left_ref,
    right_ref,
    received_hbm,
    tiles_hbm,
    cot_hbm,
    out_hbm,
    grad_hbm,
    grads_ref,
    gbias_ref,
    table,
    tiles,
    cot,
    out,
    sources,
    mean,
    grad_pre,
    inverse,
    sems,
    tile_sems,
):
    nblocks, npairs, rows, _ = tiles.shape
    width = table.shape[2]
    copies = [
        pltpu.make_async_copy(blocks_hbm, table.at[pl.ds(0, nblocks)], sems.at[0]),
        pltpu.make_async_copy(
            received_hbm, table.at[pl.ds(nblocks + 2, received_hbm.shape[0])], sems.at[1]
        ),
    ]
    tile_copies = [
        pltpu.make_async_copy(tiles_hbm.at[b], tiles.at[b], tile_sems.at[b])
        for b in range(nblocks)
    ]
    cot_copy = pltpu.make_async_copy(cot_hbm, cot, sems.at[2])
    out_copy = pltpu.make_async_copy(out, out_hbm, sems.at[3])
    grad_copy = pltpu.make_async_copy(grad_pre, grad_hbm, sems.at[4])
    for copy in copies:
        copy.start()
    for copy in tile_copies:
        copy.start()
    cot_copy.start()
    table[nblocks] = left_ref[...]
    table[nblocks + 1] = right_ref[...]
    invert_degree(degree_ref, inverse)
    for copy in copies:
        copy.wait()

    cot_copy.wait()
    w_self = w_self_ref[...]
    w_neigh = w_neigh_ref[...]
    gbias = jnp.zeros((1, width), F32)
    def aggregate(b):
        for p in range(npairs):
            sources[b % 2, pl.ds(p * rows, rows), :] = table[pairs_ref[b, p]]
        stacked = sources[b % 2]
        tile_copies[b].wait()
        summed = jnp.dot(tile_row(tiles, b), stacked, preferred_element_type=F32)
        mean[b] = by_degree(summed, inverse, b).astype(BF16)

    def activate(b, gbias):
        features = table[b : b + step].reshape(step * rows, width)
        means = mean[b : b + step].reshape(step * rows, width)
        preact = (
            jnp.dot(features, w_self, preferred_element_type=F32)
            + jnp.dot(means, w_neigh, preferred_element_type=F32)
            + bias_ref[...]
        )
        sigma = jax.nn.sigmoid(preact)
        out[b : b + step] = (preact * sigma).astype(BF16).reshape(step, rows, width)
        cots = cot[b : b + step].reshape(step * rows, width).astype(F32)
        grad = (cots * sigma * (1.0 + preact * (1.0 - sigma))).astype(BF16)
        grad_pre[pl.ds(b * rows, step * rows), :] = grad
        return gbias + jnp.sum(grad.astype(F32), axis=0, keepdims=True)

    step = 2
    for b in range(nblocks):
        aggregate(b)
    for b in range(0, nblocks, step):
        gbias = activate(b, gbias)
    grad_copy.start()
    out_copy.start()
    gbias_ref[...] = gbias

    grads = grad_pre[...]
    features = table[:nblocks].reshape(nblocks * rows, width)
    means = mean[...].reshape(nblocks * rows, width)
    grads_ref[:width, :] = lax.dot_general(
        features, grads, CONTRACT_ROWS, preferred_element_type=F32
    ).astype(BF16)
    grads_ref[width:, :] = lax.dot_general(
        means, grads, CONTRACT_ROWS, preferred_element_type=F32
    ).astype(BF16)
    grad_copy.wait()
    out_copy.wait()


def backward_kernel(
    pairs_ref,
    degree_ref,
    w_self_ref,
    w_neigh_ref,
    grad_ref,
    tiles_hbm,
    own_ref,
    rims_ref,
    slots_ref,
    tiles,
    inverse,
    entries,
    tile_sems,
):
    nblocks, npairs, rows, _ = tiles.shape
    width = w_self_ref.shape[0]
    tile_copies = [
        pltpu.make_async_copy(tiles_hbm.at[b], tiles.at[b], tile_sems.at[b])
        for b in range(nblocks)
    ]
    for copy in tile_copies:
        copy.start()
    invert_degree(degree_ref, inverse)
    entries[nblocks:] = jnp.zeros((entries.shape[0] - nblocks, rows, width), F32)
    w_self = w_self_ref[...]
    w_neigh = w_neigh_ref[...]
    own = lax.dot_general(grad_ref[...], w_self, CONTRACT_COLS, preferred_element_type=F32)
    entries[:nblocks] = own.reshape(nblocks, rows, width)
    for b in range(nblocks):
        grad = grad_ref[pl.ds(b * rows, rows), :]
        grad_mean = lax.dot_general(grad, w_neigh, CONTRACT_COLS, preferred_element_type=F32)
        grad_mean = by_degree(grad_mean, inverse, b).astype(BF16)
        tile_copies[b].wait()
        parts = lax.dot_general(
            tile_row(tiles, b), grad_mean, CONTRACT_ROWS, preferred_element_type=F32
        )
        for p in range(npairs):
            entry = pairs_ref[b, p]
            entries[entry] = entries[entry] + parts[p * rows : (p + 1) * rows]

    own_ref[...] = entries[:nblocks]
    rims_ref[...] = entries[nblocks : nblocks + 2].astype(BF16)
    slots_ref[...] = entries[nblocks + 2 :].astype(BF16)


def combine_kernel(send_ref, own_ref, returned_ref, low_ref, high_ref, out_ref, total):
    total[...] = own_ref[...]
    last = total.shape[0] - 1
    total[0] = total[0] + low_ref[...].astype(F32)
    total[last] = total[last] + high_ref[...].astype(F32)
    for j in range(returned_ref.shape[0]):
        block = send_ref[0, j]
        total[block] = total[block] + returned_ref[j].astype(F32)
    out_ref[...] = total[...].astype(BF16)


def call_forward(
    blocks, left, right, received, tiles, cot, pairs, degree, w_self, w_neigh, bias
):
    nblocks, npairs, rows, _ = tiles.shape
    width = blocks.shape[2]
    entries = nblocks + 2 + received.shape[0]
    shape = jax.ShapeDtypeStruct
    return pl.pallas_call(
        forward_kernel,
        out_shape=(
            shape(blocks.shape, BF16),
            shape((nblocks * rows, width), BF16),
            shape((2 * width, width), BF16),
            shape((1, width), F32),
        ),
        in_specs=[SMEM] + [VMEM] * 4 + [HBM, VMEM, VMEM, HBM, HBM, HBM],
        out_specs=(ANY, ANY, VMEM, VMEM),
        scratch_shapes=[
            pltpu.VMEM((entries, rows, width), BF16),
            pltpu.VMEM(tiles.shape, BF16),
            pltpu.VMEM(blocks.shape, BF16),
            pltpu.VMEM(blocks.shape, BF16),
            pltpu.VMEM((2, npairs * rows, width), BF16),
            pltpu.VMEM(blocks.shape, BF16),
            pltpu.VMEM((nblocks * rows, width), BF16),
            pltpu.VMEM((nblocks, rows, rows), F32),
            pltpu.SemaphoreType.DMA((5,)),
            pltpu.SemaphoreType.DMA((nblocks,)),
        ],
        compiler_params=params(58),
        cost_estimate=pl.CostEstimate(
            flops=2 * 10**9, bytes_accessed=6 * 10**6, transcendentals=nblocks * rows * width
        ),
    )(pairs, degree, w_self, w_neigh, bias, blocks, left, right, received, tiles, cot)


def call_backward(grad, tiles, pairs, degree, w_self, w_neigh):
    nblocks, _, rows, _ = tiles.shape
    width = w_self.shape[0]
    dom = lax.axis_size("dom")
    shape = jax.ShapeDtypeStruct
    return pl.pallas_call(
        backward_kernel,
        out_shape=(
            shape((nblocks, rows, width), F32),
            shape((2, rows, width), BF16),
            shape((dom, rows, width), BF16),
        ),
        in_specs=[SMEM] + [VMEM] * 4 + [HBM],
        out_specs=(VMEM,) * 3,
        scratch_shapes=[
            pltpu.VMEM(tiles.shape, BF16),
            pltpu.VMEM((nblocks, rows, rows), F32),
            pltpu.VMEM((nblocks + 2 + dom, rows, width), F32),
            pltpu.SemaphoreType.DMA((nblocks,)),
        ],
        compiler_params=params(58),
        cost_estimate=pl.CostEstimate(
            flops=2 * 10**9, bytes_accessed=8 * 10**6, transcendentals=0
        ),
    )(pairs, degree, w_self, w_neigh, grad, tiles)


def neighbours(low_source, high_source, axis):
    count = lax.axis_size(axis)
    forward = [(i, i + 1) for i in range(count - 1)]
    backward = [(target, source) for source, target in forward]
    return lax.ppermute(low_source, axis, forward), lax.ppermute(high_source, axis, backward)


def reduce_grads(grads, gbias, scale, beside):
    twins = lax.axis_size("mid")
    peers = lax.axis_size("dom") * twins
    inner_size = lax.axis_size(INNER)
    hidden = grads.shape[1]
    chunks = grads.reshape(inner_size, grads.shape[0] // inner_size, hidden)
    pieces = lax.all_to_all(chunks, INNER, split_axis=0, concat_axis=0, tiled=True)
    pieces, beside = lax.optimization_barrier((pieces, beside))
    rows = chunks.shape[1] * chunks.shape[2] // LANES
    spread = pl.pallas_call(
        piece_kernel,
        out_shape=jax.ShapeDtypeStruct((peers, rows + 8, LANES), BF16),
        in_specs=[VMEM, VMEM],
        out_specs=VMEM,
        compiler_params=params(),
    )(pieces, gbias)
    spread = lax.all_to_all(spread, ("dom", "mid"), split_axis=0, concat_axis=0, tiled=True)
    state = pl.pallas_call(
        functools.partial(start_kernel, scale),
        out_shape=jax.ShapeDtypeStruct((twins + 1, rows, LANES), BF16),
        in_specs=[VMEM],
        out_specs=VMEM,
        compiler_params=params(),
    )(spread)
    return state, beside


def gather_grads(state, hidden, beside):
    inner_size = lax.axis_size(INNER)
    bits = inner_size.bit_length() - 1
    groups = [(low, 1) for low in reversed(range(bits)) if low != 1]
    index = lax.axis_index(INNER).astype(jnp.int32).reshape(1)
    place = [(chunk >> 1) % 2 for chunk in range(inner_size)]
    for low, size in groups:
        count = state.shape[0] - 1
        theirs = []
        for mask in range(1, 1 << size):
            pairs = [(i, i ^ (mask << low)) for i in range(inner_size)]
            theirs.append(lax.ppermute(state, INNER, pairs))
        if low == groups[-1][0]:
            theirs, beside = lax.optimization_barrier((theirs, beside))
        place = [
            where + ((chunk >> low) % (1 << size)) * count for chunk, where in enumerate(place)
        ]
        state = pl.pallas_call(
            functools.partial(grow_kernel, low),
            out_shape=jax.ShapeDtypeStruct(((count << size) + 1,) + state.shape[1:], BF16),
            in_specs=[SMEM] + [VMEM] * (1 + len(theirs)),
            out_specs=VMEM,
            compiler_params=params(),
        )(index, state, *theirs)
    unpacked = pl.pallas_call(
        functools.partial(unpack_kernel, place),
        out_shape=(
            jax.ShapeDtypeStruct((hidden, hidden), F32),
            jax.ShapeDtypeStruct((hidden, hidden), F32),
            jax.ShapeDtypeStruct((2, LANES), F32),
        ),
        in_specs=[VMEM],
        out_specs=(VMEM,) * 3,
        compiler_params=params(),
    )(state)
    return unpacked, beside


def unpack_kernel(place, state_ref, self_ref, neigh_ref, bias_ref):
    hidden = self_ref.shape[1]
    groups = hidden // LANES
    rows = state_ref.shape[1] // groups
    half = len(place) // 2
    for chunk, where in enumerate(place):
        ref = self_ref if chunk < half else neigh_ref
        first = (chunk % half) * rows
        values = state_ref[where].astype(F32)
        for k in range(groups):
            ref[first : first + rows, k * LANES : (k + 1) * LANES] = values[
                k * rows : (k + 1) * rows
            ]
    tail = state_ref[len(place)].astype(F32)
    bias_ref[...] = tail[:groups] + tail[groups : 2 * groups]


def per_device(
    features, tiles, pair_source, in_degree, send_blocks, w_self, w_neigh, bias, cotangent
):
    rows_dev, width = features.shape
    nblocks, _, rows, _ = tiles.shape
    dom_size = lax.axis_size("dom")
    blocks = features.reshape(nblocks, rows, width)
    outgoing = pl.pallas_call(
        pick_kernel,
        out_shape=jax.ShapeDtypeStruct((dom_size, rows, width), BF16),
        in_specs=[SMEM, HBM],
        out_specs=VMEM,
        scratch_shapes=[pltpu.SemaphoreType.DMA((dom_size,))],
        compiler_params=params(58),
    )(send_blocks, blocks)
    received = lax.all_to_all(outgoing, "dom", split_axis=0, concat_axis=0, tiled=True)
    left, right = neighbours(blocks[nblocks - 1], blocks[0], INNER)
    degree = in_degree.reshape(nblocks, rows)
    layer_out, grad_pre, grads, gbias = call_forward(
        blocks,
        left,
        right,
        received,
        tiles,
        cotangent.reshape(nblocks, rows, width),
        pair_source,
        degree,
        w_self,
        w_neigh,
        bias[None, :],
    )
    own, rims, slots = call_backward(grad_pre, tiles, pair_source, degree, w_self, w_neigh)
    scale = 1.0 / math.sqrt(rows_dev * dom_size * lax.axis_size(INNER))
    state, (own, rims, slots) = reduce_grads(grads, gbias, scale, (own, rims, slots))
    low, high = neighbours(rims[1], rims[0], INNER)
    state, slots, low, high = lax.optimization_barrier((state, slots, low, high))
    returned = lax.all_to_all(slots, "dom", split_axis=0, concat_axis=0, tiled=True)
    grad_features = pl.pallas_call(
        combine_kernel,
        out_shape=jax.ShapeDtypeStruct(blocks.shape, BF16),
        in_specs=[SMEM] + [VMEM] * 4,
        out_specs=VMEM,
        scratch_shapes=[pltpu.VMEM(blocks.shape, F32)],
        compiler_params=params(),
        cost_estimate=pl.CostEstimate(
            flops=10**6, bytes_accessed=3 * 10**6, transcendentals=0
        ),
    )(send_blocks, own, returned, low, high)
    (sum_self, sum_neigh, sum_bias), grad_features = gather_grads(state, width, grad_features)
    return (
        layer_out.reshape(rows_dev, width),
        grad_features.reshape(rows_dev, width),
        sum_self,
        sum_neigh,
        sum_bias.reshape(-1),
    )


def solution(mesh):
    devices = mesh.devices.reshape(mesh.shape["dom"], -1, 2, 2)
    return jax.shard_map(
        per_device,
        mesh=Mesh(devices, ALL),
        in_specs=(
            P(ALL, None),
            P(ALL, None, None, None),
            P(ALL, None),
            P(ALL),
            P(ALL, None),
            P(),
            P(),
            P(),
            P(ALL, None),
        ),
        out_specs=(P(ALL, None), P(ALL, None), P(), P(), P()),
        check_vma=False,
    )
```
